32 devices in a mesh: ens: 2 (over y), lon: 16 (over z, x, core).
Axes of the slice: x: 2, y: 2, z: 4, core: 2. Of those that a mesh axis runs over, the one named last changes fastest.
Arguments:
- final_cot: float32 [10, 256, 2048], P('ens', 'lon'), parts along dimension 0, may hold values from -6 to 6
- strains: bfloat16 [16, 3, 256, 2048], P('ens', None, 'lon'), parts along dimension 0, may hold values from -6 to 6
- strength: float32 [256, 2048], P('lon'), may hold values from 0.25 to 1
- mass: float32 [256, 2048], P('lon'), may hold values from 1 to 4
- ice_mask: int32 [256, 2048], P('lon'), may hold values 0 or 1
- partner: int32 [256], P('lon'), may hold values from 0 to 255, as said below
Outputs:
- initial_cot: float32 [10, 256, 2048], P('ens', 'lon'), parts along dimension 0
The draws below stay inside these ranges and needn't reach their ends.
There are 2 independent parts, one for each index of `ens`. The reference program is written for one: setup_inputs(seed, part) draws one part's arguments, and reference() takes and returns one part's arrays. A program takes and returns all parts, laid end to end along the dimension named above; an argument that names none is the same for every part. Nothing has to cross between parts.
Inputs may be any that keep to these rules, and one draw needn't show every extreme that they name: Columns form 256 // 16 aligned blocks of 16; the partners of the columns of block b are exactly the columns of block 15 - b, and the partner of a column's partner is the column itself.
All inputs are finite; a program needn't handle non-finite values. No bound on the sum of `ice_mask` on one device may be relied on, other than what follows from the above.
Results may differ from the reference program's by a relative error of at most 0.0003.
Values may be sent and summed in bfloat16 or wider, within the bound.
No kernel may reach another device: no remote copies, remote signals or barrier semaphores. Data moves between devices by JAX's collectives and lax.ppermute only.
A program may use at most 64 MiB of HBM per device.

```python
import math
import jax
import jax.numpy as jnp

LON_DEV = 16
NLAT = 2048
SUB = 8
NLON = 256


def draw_partner(key, part):
    key = jax.random.fold_in(key, 5)
    blocks = NLON // LON_DEV
    half = blocks // 2
    keys = jax.random.split(key, half)
    perms = jax.vmap(lambda single: jax.random.permutation(single, LON_DEV))(keys).astype(jnp.int32)
    inverse = jnp.argsort(perms, axis=1, stable=True).astype(jnp.int32)
    lower = (blocks - 1 - jnp.arange(half, dtype=jnp.int32))[:, None] * LON_DEV + perms
    upper = jnp.arange(half, dtype=jnp.int32)[:, None] * LON_DEV + inverse
    return jnp.concatenate([lower.reshape(-1), upper[::-1].reshape(-1)]).astype(jnp.int32)


def plant(drawn, stream_key, smallest, top_value):
    dims = drawn.shape
    place = [jax.random.randint(jax.random.fold_in(stream_key, axis), (), 0, dims[axis]) for axis in range(len(dims))]
    drawn = drawn.at[tuple(place)].set(smallest)
    longest = dims.index(max(dims))
    place[longest] = (place[longest] + 1) % dims[longest]
    return drawn.at[tuple(place)].set(top_value)


def block_scale(stream_key, extent, shards, smallest, top_value):
    factor_of = 1.0
    for dim, shards_of in shards:
        heights = jax.random.uniform(jax.random.fold_in(jax.random.fold_in(stream_key, 6), dim), (shards_of,), jnp.float32, smallest / len(shards), top_value / len(shards))
        factor_of = factor_of * jnp.repeat(jnp.exp(heights), extent[dim] // shards_of).reshape((-1,) + (1,) * (len(extent) - 1 - dim))
    return factor_of


def bell_draw(stream_key, dims, width, bound, cuts=(), held_as=jnp.bfloat16):
    gain = block_scale(stream_key, dims, cuts, -0.22, 0.18) if cuts else 1.0
    values = jax.random.normal(stream_key, dims, jnp.float32) * width * gain
    return jnp.minimum(jnp.maximum(values, -bound), bound).astype(held_as)


def setup_inputs(seed: int = 0, part: int = 0) -> dict:
    key_list = jax.random.split(jax.random.key(seed), 7)
    part_splits = jax.random.split(jax.random.fold_in(key_list[6], part), 7)
    return {
        "final_cot": bell_draw(part_splits[0], (5, NLON, NLAT), 1.0, 6.0, ((1, 16),), jnp.float32),
        "strains": bell_draw(part_splits[1], (SUB, 3, NLON, NLAT), 1.0, 6.0, ((2, 16),)),
        "strength": jnp.clip(jnp.exp(math.log(1.0) - 1.3862944 * jax.random.uniform(key_list[2], (NLON, NLAT), jnp.float32) ** block_scale(key_list[2], (NLON, NLAT), ((0, 16),), -0.2, 0.2)), 0.25, 1.0),
        "mass": jnp.clip(jnp.exp(math.log(4.0) - 1.3862944 * jax.random.uniform(key_list[3], (NLON, NLAT), jnp.float32) ** block_scale(key_list[3], (NLON, NLAT), ((0, 16),), -0.2, 0.2)), 1.0, 4.0),
        "ice_mask": plant((jax.random.randint(key_list[4], (NLON, NLAT), 0, 4) < 3).astype(jnp.int32), jax.random.fold_in(key_list[4], 1), 0, 1),
        "partner": draw_partner(jax.random.fold_in(key_list[6], 71), part),
    }


relax_keep = 5.0 / 6.0
relax_take = 1.0 / 6.0
inertia = 5.0
coriolis = 0.5
delta_floor = 0.5
ellipse_inv = 0.25

def viscosity(saved, strength):
    rates = saved.astype(jnp.float32)
    delta = jnp.sqrt(rates[0] * rates[0] + ellipse_inv * (rates[1] * rates[1] + rates[2] * rates[2]))
    zeta = strength / (2.0 * jnp.maximum(delta, delta_floor))
    return (zeta, ellipse_inv * zeta)

def below(field):
    return jnp.concatenate([jnp.zeros_like(field[:, :1]), field[:, :-1]], axis=1)

def subcycle(state, zeta, eta, wet, mass, partner):
    vel_u, vel_v = (state[0], state[1])
    grad_ux = jnp.roll(vel_u, -1, 0) - vel_u
    grad_vx = jnp.roll(vel_v, -1, 0) - vel_v
    grad_uy = vel_u - below(vel_u)
    grad_vy = vel_v - below(vel_v)
    new_one = relax_keep * state[2] + relax_take * zeta * (grad_ux + grad_vy)
    new_two = relax_keep * state[3] + relax_take * eta * (grad_ux - grad_vy)
    new_shear = relax_keep * state[4] + relax_take * eta * (grad_uy + grad_vx)
    total = new_one + new_two
    differ = new_one - new_two
    fold_differ = jnp.take(differ[:, -1], partner)
    fold_shear = -jnp.take(new_shear[:, -1], partner)
    force_x = 0.5 * (total - jnp.roll(total, 1, 0)) + (jnp.concatenate([new_shear[:, 1:], fold_shear[:, None]], 1) - new_shear)
    force_y = 0.5 * (jnp.concatenate([differ[:, 1:], fold_differ[:, None]], 1) - differ) + (new_shear - jnp.roll(new_shear, 1, 0))
    out_u = wet * (inertia * vel_u + force_x / mass + coriolis * vel_v) / (1.0 + inertia)
    out_v = wet * (inertia * vel_v + force_y / mass - coriolis * vel_u) / (1.0 + inertia)
    return jnp.stack([out_u, out_v, new_one, new_two, new_shear])

def reference(final_cot, strains, strength, mass, ice_mask, partner):
    wet = ice_mask.astype(jnp.float32)
    adjoint = final_cot
    anchor = jnp.zeros_like(final_cot)
    for cycle_at in reversed(range(SUB)):
        zeta, eta = viscosity(strains[cycle_at], strength)
        _, pull = jax.vjp(lambda state: subcycle(state, zeta, eta, wet, mass, partner), anchor)
        adjoint = pull(adjoint)[0]
    return adjoint
```

```python
import functools

import jax
import jax.numpy as jnp
from jax import lax
from jax.experimental import pallas as pl
from jax.experimental.pallas import tpu as pltpu
from jax.sharding import PartitionSpec as P

COLS = 16
STEPS = 8
HALO = 8
TILE = 16
LANES = 128
GROUPS = 16
EXT = 40
UNROLL = 4

WEST_WIDTH = [STEPS + 1 - step for step in range(1, STEPS + 1)]
EAST_WIDTH = [STEPS - step for step in range(1, STEPS + 1)]
WEST_FIELD = [0, 8, 16, 24, 32]
WEST_COUNT = [8, 8, 8, 8, 8]
WEST_MASS = 40
WEST_ZETA = [48 + sum(WEST_WIDTH[:k]) for k in range(STEPS)]
WEST_SIZE = 48 + sum(WEST_WIDTH)
EAST_FIELD = [0, 8, 16, 23, 30]
EAST_COUNT = [8, 8, 7, 7, 7]
EAST_MASS = 37
EAST_ZETA = [45 + sum(EAST_WIDTH[:k]) for k in range(STEPS)]
EAST_SIZE = 45 + sum(EAST_WIDTH)
STRIP_FIELDS = 13
SHRINK = (5.0 / 6.0) ** STEPS


def as_rows(field):
    lead = field.shape[:-2]
    tiled = field.reshape(lead + (2, 8, GROUPS, LANES)).swapaxes(-3, -2)
    return tiled.reshape(lead + (2 * GROUPS * 8, LANES))


def from_rows(field):
    lead = field.shape[:-2]
    tiled = field.reshape(lead + (2, GROUPS, 8, LANES)).swapaxes(-3, -2)
    return tiled.reshape(lead + (COLS, GROUPS * LANES))


def column_slices(col):
    start = (col // 8) * 128 + col % 8
    return pl.ds(start, 8, 16), pl.ds(start + 8, 8, 16)


def column_tile(load, col):
    even, odd = column_slices(col)
    return jnp.concatenate([load(even), load(odd)], axis=0)


def pack_kernel(
    state, strains, strength, mass, ice_mask, partner,
    west_out, east_out, strip_out, zeta_out, mass_out, rows,
):
    lane = lax.broadcasted_iota(jnp.int32, (COLS, LANES), 1)
    strip = jnp.zeros((COLS, LANES), jnp.float32)

    def strip_field(strip, at, tile):
        moved = pltpu.roll(tile, (8 * at + 8) % LANES, 1)
        return jnp.where((lane >= 8 * at) & (lane < 8 * at + 8), moved, strip)

    for field in range(5):
        for col in range(COLS):
            tile = column_tile(lambda at: state[field, at, :], col).astype(jnp.bfloat16)
            if col >= 8:
                west_out[WEST_FIELD[field] + col - 8] = tile
            elif col < EAST_COUNT[field]:
                east_out[EAST_FIELD[field] + col] = tile
        last = jnp.concatenate([state[field, 120:128, :], state[field, 248:256, :]], 0)
        strip = strip_field(strip, field, last)

    for group in range(GROUPS):
        at = slice(128 * group, 128 * group + 128)
        weight = ice_mask[:, at].astype(jnp.float32) / (6.0 * mass[:, at])
        rows[8 * group : 8 * group + 8] = weight[:8]
        rows[128 + 8 * group : 136 + 8 * group] = weight[8:]
        if group == GROUPS - 1:
            strip = strip_field(strip, 5, weight)
    for col in range(COLS):
        tile = column_tile(lambda at: rows[at, :], col)
        mass_out[col] = tile
        if col >= 8:
            west_out[WEST_MASS + col - 8] = tile.astype(jnp.bfloat16)
        else:
            east_out[EAST_MASS + col] = tile.astype(jnp.bfloat16)

    for step in range(STEPS):
        cycle = STEPS - 1 - step
        for group in range(GROUPS):
            at = slice(128 * group, 128 * group + 128)
            div = strains[cycle, 0, :, at].astype(jnp.float32)
            ten = strains[cycle, 1, :, at].astype(jnp.float32)
            she = strains[cycle, 2, :, at].astype(jnp.float32)
            square = div * div + 0.25 * (ten * ten + she * she)
            zeta = (0.05 * strength[:, at]) * lax.rsqrt(jnp.maximum(square, 0.25))
            rows[8 * group : 8 * group + 8] = zeta[:8]
            rows[128 + 8 * group : 136 + 8 * group] = zeta[8:]
            if group == GROUPS - 1 and step < STEPS - 1:
                strip = strip_field(strip, 6 + step, zeta)
        for col in range(COLS):
            tile = column_tile(lambda at: rows[at, :], col)
            zeta_out[step, col] = tile
            if col >= COLS - WEST_WIDTH[step]:
                west_out[WEST_ZETA[step] + col - (COLS - WEST_WIDTH[step])] = tile.astype(jnp.bfloat16)
            if col < EAST_WIDTH[step]:
                east_out[EAST_ZETA[step] + col] = tile.astype(jnp.bfloat16)

    row_at = lax.broadcasted_iota(jnp.int32, (COLS, LANES), 0)
    place = jnp.zeros((COLS, LANES), jnp.int32)
    for col in range(COLS):
        place = jnp.where(row_at == col, lax.rem(partner[col], COLS), place)
    strip = jnp.where(lane == 8 * STRIP_FIELDS, place.astype(jnp.float32), strip)
    packed = strip.astype(jnp.bfloat16)
    for device in range(strip_out.shape[0]):
        strip_out[device] = packed


def fold_values(strips, folds):
    total = strips.shape[0]
    count = total // LANES
    lane = lax.broadcasted_iota(jnp.int32, (8, LANES), 1)
    sub = lax.broadcasted_iota(jnp.int32, (8, total), 0)
    turned = [strips[LANES * r : LANES * r + LANES, :].astype(jnp.float32).T for r in range(count)]

    def field(at):
        return jnp.concatenate([part[8 * at : 8 * at + 8] for part in turned], axis=1)

    places = [
        (7 - lane // COLS) * COLS
        + jnp.broadcast_to(part[8 * STRIP_FIELDS : 8 * STRIP_FIELDS + 1], (8, LANES)).astype(jnp.int32)
        for part in turned
    ]

    def by_partner(value):
        parts = [
            jnp.take_along_axis(
                value[:, LANES * (count - 1 - r) : LANES * (count - r)], places[r], axis=1,
                mode="promise_in_bounds",
            )
            for r in range(count)
        ]
        return jnp.concatenate(parts, axis=1)

    def next_col(value):
        return pltpu.roll(value, total - 1, 1)

    def prev_col(value):
        return pltpu.roll(value, 1, 1)

    def row_above(value):
        return jnp.where(sub == 7, 0.0, pltpu.roll(value, 7, 0))

    def row_below(value):
        return pltpu.roll(value, 1, 0)

    vel_u, vel_v, one, two, shear, weight = (field(at) for at in range(6))
    one = 2.0 * one
    two = 2.0 * two
    wet = weight != 0.0
    fold_p = jnp.zeros((8, total), jnp.float32)
    fold_q = jnp.zeros((8, total), jnp.float32)
    for step in range(STEPS):
        p = weight * vel_u
        q = weight * vel_v
        far_p = by_partner(p)
        far_q = by_partner(q)
        turn = (step + 1) % 8
        fold_p = jnp.where(sub == step, pltpu.roll(far_p, turn, 0) if turn else far_p, fold_p)
        fold_q = jnp.where(sub == step, pltpu.roll(far_q, turn, 0) if turn else far_q, fold_q)
        if step == STEPS - 1:
            break
        far_p = jnp.where(sub == 7, far_p, 0.0)
        far_q = jnp.where(sub == 7, far_q, 0.0)
        along = p - next_col(p)
        across = row_below(q) - q + far_q
        one = one + (along + across)
        two = two + (along - across)
        shear = shear + (row_below(p) - p - far_p) + (q - next_col(q))
        zeta = field(6 + step)
        first = zeta * one
        second = (0.25 * zeta) * two
        third = (0.5 * zeta) * shear
        x = first + second
        y = first - second
        wet_u = jnp.where(wet, vel_u, 0.0)
        wet_v = jnp.where(wet, vel_v, 0.0)
        vel_u = (wet_u - 0.1 * wet_v) + (prev_col(x) - x) + (third - row_above(third))
        vel_v = (wet_v + 0.1 * wet_u) + (prev_col(third) - third) + (y - row_above(y))

    me = lax.axis_index("lon")
    shift = lax.rem(2 * total + HALO - COLS * me, total)
    both = jnp.concatenate(
        [pltpu.roll(fold_p, shift, 1)[:, :LANES], pltpu.roll(fold_q, shift, 1)[:, :LANES]], axis=0
    )
    tall = jnp.concatenate([both, jnp.zeros((LANES - 16, LANES), jnp.float32)], axis=0).T
    for at in range(16):
        folds[at] = pltpu.roll(tall[:EXT], LANES - 1 - at, 1)


def main_kernel(
    state, zeta_in, mass_in, west, east, strips, out,
    vel_u, vel_v, one, two, shear, weight, zeta, folds,
):
    fields = (vel_u, vel_v, one, two, shear)
    scales = (1.0, 1.0, 2.0, 2.0, 1.0)
    fold_values(strips, folds)
    for field in range(5):
        for col in range(COLS):
            tile = column_tile(lambda at: state[field, at, :], col)
            fields[field][HALO + col] = scales[field] * tile
        for col in range(WEST_COUNT[field]):
            fields[field][col] = scales[field] * west[WEST_FIELD[field] + col].astype(jnp.float32)
        for col in range(EAST_COUNT[field]):
            fields[field][HALO + COLS + col] = scales[field] * east[EAST_FIELD[field] + col].astype(jnp.float32)
    for col in range(8):
        weight[col] = west[WEST_MASS + col].astype(jnp.float32)
        weight[HALO + COLS + col] = east[EAST_MASS + col].astype(jnp.float32)
    for col in range(COLS):
        weight[HALO + col] = mass_in[col]
    for step in range(STEPS):
        for col in range(COLS):
            zeta[step, HALO + col] = zeta_in[step, col]
        for col in range(WEST_WIDTH[step]):
            zeta[step, HALO - WEST_WIDTH[step] + col] = west[WEST_ZETA[step] + col].astype(jnp.float32)
        for col in range(EAST_WIDTH[step]):
            zeta[step, HALO + COLS + col] = east[EAST_ZETA[step] + col].astype(jnp.float32)

    lane = lax.broadcasted_iota(jnp.int32, (8, LANES), 1)
    sub = lax.broadcasted_iota(jnp.int32, (8, LANES), 0)
    first_lane = lane == 0
    last_lane = lane == LANES - 1
    top = sub == 0
    bottom = sub == 7
    corner = last_lane & bottom

    def row_above(value):
        turned = pltpu.roll(value, LANES - 1, 1)
        even, odd = turned[:8], turned[8:]
        carried = jnp.where(bottom, 0.0, pltpu.roll(even, 7, 0))
        return jnp.concatenate([jnp.where(last_lane, odd, even), jnp.where(last_lane, carried, odd)], 0)

    def row_below(value):
        turned = pltpu.roll(value, 1, 1)
        even, odd = turned[:8], turned[8:]
        carried = jnp.where(top, 0.0, pltpu.roll(odd, 1, 0))
        return jnp.concatenate([jnp.where(first_lane, carried, even), jnp.where(first_lane, even, odd)], 0)

    def at_fold(value, add):
        return jnp.concatenate([value[:8], value[8:] + jnp.where(corner, add, 0.0)], 0)

    def forces(col):
        u, v, w = vel_u[col], vel_v[col], weight[col]
        wet = w != 0.0
        wet_u = jnp.where(wet, u, 0.0)
        wet_v = jnp.where(wet, v, 0.0)
        return w * u, w * v, wet_u - 0.1 * wet_v, wet_v + 0.1 * wet_u

    blank = jnp.zeros((TILE, LANES), jnp.float32)

    @pl.loop(0, STEPS)
    def _(step):
        begin = step
        groups = (2 * STEPS + COLS - 1 - 2 * step + UNROLL - 1) // UNROLL

        def body(group, carry):
            p, q, keep_u, keep_v, west_x, west_c = carry
            for part in range(UNROLL):
                col = begin + group * UNROLL + part
                next_p, next_q, next_u, next_v = forces(col + 1)
                along = p - next_p
                across = at_fold(row_below(q) - q, folds[8 + step, pl.ds(col, 1), :])
                turn = at_fold(row_below(p) - p, -folds[step, pl.ds(col, 1), :])
                new_one = one[col] + (along + across)
                new_two = two[col] + (along - across)
                new_shear = shear[col] + turn + (q - next_q)
                one[col] = new_one
                two[col] = new_two
                shear[col] = new_shear
                z = zeta[step, col]
                first = z * new_one
                second = (0.25 * z) * new_two
                c = (0.5 * z) * new_shear
                x = first + second
                y = first - second
                vel_u[col] = keep_u + (west_x - x) + (c - row_above(c))
                vel_v[col] = keep_v + (west_c - c) + (y - row_above(y))
                p, q, keep_u, keep_v, west_x, west_c = next_p, next_q, next_u, next_v, x, c
            return p, q, keep_u, keep_v, west_x, west_c

        lax.fori_loop(0, groups, body, forces(begin) + (blank, blank))

    outs = (SHRINK, SHRINK, 0.5 * SHRINK, 0.5 * SHRINK, SHRINK)
    for field in range(5):
        for col in range(COLS):
            tile = outs[field] * fields[field][HALO + col]
            even, odd = column_slices(col)
            out[field, even, :] = tile[:8]
            out[field, odd, :] = tile[8:]


def on_device(final_cot, strains, strength, mass, ice_mask, partner):
    count = lax.axis_size("lon")
    state = as_rows(final_cot)
    whole = pl.BlockSpec(memory_space=pltpu.VMEM)
    f32 = jnp.float32
    bf16 = jnp.bfloat16
    params = pltpu.CompilerParams(vmem_limit_bytes=48 * 1024 * 1024)
    west_send, east_send, strip_send, zeta, weight = pl.pallas_call(
        pack_kernel,
        out_shape=(
            jax.ShapeDtypeStruct((WEST_SIZE, TILE, LANES), bf16),
            jax.ShapeDtypeStruct((EAST_SIZE, TILE, LANES), bf16),
            jax.ShapeDtypeStruct((count, COLS, LANES), bf16),
            jax.ShapeDtypeStruct((STEPS, COLS, TILE, LANES), f32),
            jax.ShapeDtypeStruct((COLS, TILE, LANES), f32),
        ),
        in_specs=[whole] * 5 + [pl.BlockSpec(memory_space=pltpu.SMEM)],
        out_specs=(whole,) * 5,
        scratch_shapes=[pltpu.VMEM((256, LANES), f32)],
        compiler_params=params,
    )(state, strains, strength, mass, ice_mask, partner)

    west = lax.ppermute(west_send, "lon", [(i, (i + 1) % count) for i in range(count)])
    east = lax.ppermute(east_send, "lon", [(i, (i - 1) % count) for i in range(count)])
    strips = lax.all_to_all(strip_send, "lon", 0, 0, tiled=True).reshape(count * COLS, LANES)

    out = pl.pallas_call(
        main_kernel,
        out_shape=jax.ShapeDtypeStruct(state.shape, f32),
        in_specs=[whole] * 6,
        out_specs=whole,
        scratch_shapes=[pltpu.VMEM((EXT, TILE, LANES), f32)] * 6
        + [pltpu.VMEM((STEPS, EXT, TILE, LANES), f32), pltpu.VMEM((16, EXT, LANES), f32)],
        compiler_params=params,
    )(state, zeta, weight, west, east, strips)
    return from_rows(out)


def solution(mesh):
    return jax.shard_map(
        on_device,
        mesh=mesh,
        in_specs=(
            P("ens", "lon", None),
            P("ens", None, "lon", None),
            P("lon", None),
            P("lon", None),
            P("lon", None),
            P("lon"),
        ),
        out_specs=P("ens", "lon", None),
        check_vma=False,
    )
```

```python
import functools

import jax
import jax.numpy as jnp
from jax import lax
from jax.experimental import pallas as pl
from jax.experimental.pallas import tpu as pltpu
from jax.sharding import PartitionSpec as P

COLS = 16
STEPS = 8
HALO = 8
TILE = 16
LANES = 128
GROUPS = 16
EXT = 40
UNROLL = 16

WEST_WIDTH = [STEPS + 1 - step for step in range(1, STEPS + 1)]
EAST_WIDTH = [STEPS - step for step in range(1, STEPS + 1)]
WEST_FIELD = [0, 8, 16, 24, 32]
WEST_COUNT = [8, 8, 8, 8, 8]
WEST_MASS = 40
WEST_ZETA = [48 + sum(WEST_WIDTH[:k]) for k in range(STEPS)]
WEST_SIZE = 48 + sum(WEST_WIDTH)
EAST_FIELD = [0, 8, 16, 23, 30]
EAST_COUNT = [8, 8, 7, 7, 7]
EAST_MASS = 37
EAST_ZETA = [45 + sum(EAST_WIDTH[:k]) for k in range(STEPS)]
EAST_SIZE = 45 + sum(EAST_WIDTH)
STRIP_FIELDS = 13
SHRINK = (5.0 / 6.0) ** STEPS


def as_rows(field):
    lead = field.shape[:-2]
    tiled = field.reshape(lead + (2, 8, GROUPS, LANES)).swapaxes(-3, -2)
    return tiled.reshape(lead + (2 * GROUPS * 8, LANES))


def from_rows(field):
    lead = field.shape[:-2]
    tiled = field.reshape(lead + (2, GROUPS, 8, LANES)).swapaxes(-3, -2)
    return tiled.reshape(lead + (COLS, GROUPS * LANES))


def column_slices(col, half):
    start = half * 128 + col
    return pl.ds(start, 8, 16), pl.ds(start + 8, 8, 16)


def column_tile(load, col, half):
    even, odd = column_slices(col, half)
    return jnp.concatenate([load(even), load(odd)], axis=0)


def west_slot(step):
    return 48 + STEPS * step - (step * (step - 1)) // 2


def east_slot(step):
    return 45 + (STEPS - 1) * step - (step * (step - 1)) // 2


def pack_kernel(
    state_hbm, strains_hbm, strength_hbm, mass_hbm, mask_hbm, partner_hbm,
    west_out, east_out, strip_out, state_out, zeta_out, mass_out,
    state, strains, strength, mass, mask, partner, rows, sems,
):
    bf16 = jnp.bfloat16
    copies = [
        pltpu.make_async_copy(strength_hbm, strength, sems.at[0]),
        pltpu.make_async_copy(partner_hbm, partner, sems.at[4]),
    ]
    strain_copies = [
        pltpu.make_async_copy(strains_hbm.at[2 * k : 2 * k + 2], strains.at[2 * k : 2 * k + 2], sems.at[5 + k])
        for k in range(STEPS // 2)
    ]
    state_copy = pltpu.make_async_copy(state_hbm, state, sems.at[3])
    cell_copies = [
        pltpu.make_async_copy(mass_hbm, mass, sems.at[1]),
        pltpu.make_async_copy(mask_hbm, mask, sems.at[2]),
    ]
    for copy in [state_copy, *copies, *strain_copies, *cell_copies]:
        copy.start()

    lane = lax.broadcasted_iota(jnp.int32, (COLS, LANES), 1)

    def strip_field(strip, at, tile):
        moved = pltpu.roll(tile, (8 * at + 8) % LANES, 1)
        return jnp.where((lane >= 8 * at) & (lane < 8 * at + 8), moved, strip)

    state_copy.wait()

    @pl.loop(0, 8)
    def _(turn):
        at = 7 - turn
        for field in range(5):
            tile = column_tile(lambda part: state[field, part, :], at, 0)
            state_out[field, HALO + at] = tile
            east_out[EAST_FIELD[field] + at] = tile.astype(bf16)
            tile = column_tile(lambda part: state[field, part, :], at, 1)
            state_out[field, HALO + 8 + at] = tile
            west_out[WEST_FIELD[field] + at] = tile.astype(bf16)

    strip = jnp.zeros((COLS, LANES), jnp.float32)
    for field in range(5):
        last = jnp.concatenate([state[field, 120:128, :], state[field, 248:256, :]], 0)
        strip = strip_field(strip, field, last)

    for copy in copies:
        copy.wait()

    def cycle_zeta(cycle, step, strip, rows):
        for group in range(GROUPS):
            at = slice(128 * group, 128 * group + 128)
            div = strains[cycle, 0, :, at].astype(jnp.float32)
            ten = strains[cycle, 1, :, at].astype(jnp.float32)
            she = strains[cycle, 2, :, at].astype(jnp.float32)
            square = div * div + 0.25 * (ten * ten + she * she)
            zeta = (0.1 * strength[:, at]) * lax.rsqrt(jnp.maximum(square, 0.25))
            rows[8 * group : 8 * group + 8] = zeta[:8]
            rows[128 + 8 * group : 136 + 8 * group] = zeta[8:]
            if group == GROUPS - 1:
                strip = strip_field(strip, 6 + step, zeta)
        for at in range(8):
            tile = column_tile(lambda part: rows[part, :], at, 0)
            zeta_out[step, HALO + at] = tile
            east_out[east_slot(step) + (EAST_WIDTH[0] - 1 - step) - at] = tile.astype(bf16)
            tile = column_tile(lambda part: rows[part, :], at, 1)
            zeta_out[step, HALO + 8 + at] = tile
            west_out[west_slot(step) + at - step] = tile.astype(bf16)
        return strip

    def two_cycles(turn, strip):
        pltpu.make_async_copy(
            strains_hbm.at[pl.ds(2 * turn, 2)], strains.at[pl.ds(2 * turn, 2)], sems.at[5 + turn]
        ).wait()
        for part in range(2):
            cycle = 2 * turn + part
            strip = cycle_zeta(cycle, STEPS - 1 - cycle, strip, rows.at[part])
        return strip

    strip = lax.fori_loop(0, STEPS // 2, two_cycles, strip)

    for copy in cell_copies:
        copy.wait()
    for group in range(GROUPS):
        at = slice(128 * group, 128 * group + 128)
        weight = mask[:, at].astype(jnp.float32) / (6.0 * mass[:, at])
        rows[0, 8 * group : 8 * group + 8] = weight[:8]
        rows[0, 128 + 8 * group : 136 + 8 * group] = weight[8:]
        if group == GROUPS - 1:
            strip = strip_field(strip, 5, weight)
    for at in range(8):
        tile = column_tile(lambda part: rows[0, part, :], at, 0)
        mass_out[HALO + at] = tile
        east_out[EAST_MASS + at] = tile.astype(bf16)
        tile = column_tile(lambda part: rows[0, part, :], at, 1)
        mass_out[HALO + 8 + at] = tile
        west_out[WEST_MASS + at] = tile.astype(bf16)

    row_at = lax.broadcasted_iota(jnp.int32, (COLS, LANES), 0)
    place = jnp.zeros((COLS, LANES), jnp.int32)
    for col in range(COLS):
        place = jnp.where(row_at == col, lax.rem(partner[col], COLS), place)
    strip = jnp.where(lane == 8 * STRIP_FIELDS, place.astype(jnp.float32), strip)
    packed = strip.astype(bf16)
    for device in range(strip_out.shape[0]):
        strip_out[device] = packed


def fold_values(strips, folds):
    total = strips.shape[0]
    count = total // LANES
    lane = lax.broadcasted_iota(jnp.int32, (8, LANES), 1)
    sub = lax.broadcasted_iota(jnp.int32, (8, total), 0)
    turned = [strips[LANES * r : LANES * r + LANES, :].astype(jnp.float32).T for r in range(count)]

    def field(at):
        return jnp.concatenate([part[8 * at : 8 * at + 8] for part in turned], axis=1)

    places = [
        (7 - lane // COLS) * COLS
        + jnp.broadcast_to(part[8 * STRIP_FIELDS : 8 * STRIP_FIELDS + 1], (8, LANES)).astype(jnp.int32)
        for part in turned
    ]

    def by_partner(value):
        parts = [
            jnp.take_along_axis(
                value[:, LANES * (count - 1 - r) : LANES * (count - r)], places[r], axis=1,
                mode="promise_in_bounds",
            )
            for r in range(count)
        ]
        return jnp.concatenate(parts, axis=1)

    def next_col(value):
        return pltpu.roll(value, total - 1, 1)

    def prev_col(value):
        return pltpu.roll(value, 1, 1)

    def row_above(value):
        return jnp.where(sub == 7, 0.0, pltpu.roll(value, 7, 0))

    def row_below(value):
        return pltpu.roll(value, 1, 0)

    vel_u, vel_v, one, two, shear, weight = (field(at) for at in range(6))
    wet = weight != 0.0
    fold_p = jnp.zeros((8, total), jnp.float32)
    fold_q = jnp.zeros((8, total), jnp.float32)
    for step in range(STEPS):
        p = weight * vel_u
        q = weight * vel_v
        far_p = by_partner(p)
        far_q = by_partner(q)
        turn = (step + 1) % 8
        fold_p = jnp.where(sub == step, pltpu.roll(far_p, turn, 0) if turn else far_p, fold_p)
        fold_q = jnp.where(sub == step, pltpu.roll(far_q, turn, 0) if turn else far_q, fold_q)
        if step == STEPS - 1:
            break
        far_p = jnp.where(sub == 7, far_p, 0.0)
        far_q = jnp.where(sub == 7, far_q, 0.0)
        along = 0.5 * (p - next_col(p))
        across = 0.5 * (row_below(q) - q + far_q)
        one = one + (along + across)
        two = two + (along - across)
        shear = shear + (row_below(p) - p - far_p) + (q - next_col(q))
        zeta = field(6 + step)
        first = zeta * one
        second = (0.25 * zeta) * two
        third = (0.25 * zeta) * shear
        x = first + second
        y = first - second
        wet_u = jnp.where(wet, vel_u, 0.0)
        wet_v = jnp.where(wet, vel_v, 0.0)
        vel_u = (wet_u - 0.1 * wet_v) + (prev_col(x) - x) + (third - row_above(third))
        vel_v = (wet_v + 0.1 * wet_u) + (prev_col(third) - third) + (y - row_above(y))

    me = lax.axis_index("lon")
    shift = lax.rem(2 * total + HALO - COLS * me, total)
    both = jnp.concatenate(
        [pltpu.roll(fold_p, shift, 1)[:, :LANES], pltpu.roll(fold_q, shift, 1)[:, :LANES]], axis=0
    )
    tall = jnp.concatenate([both, jnp.zeros((LANES - 16, LANES), jnp.float32)], axis=0).T
    for at in range(16):
        folds[at] = pltpu.roll(tall[:EXT], LANES - 1 - at, 1)


def main_kernel(west, east, strips, state_in, zeta_in, mass_in, out, state, zeta, weight, folds):
    vel_u, vel_v, one, two, shear = (state.at[field] for field in range(5))
    fold_values(strips, folds)

    @pl.loop(0, 8)
    def _(at):
        for field in range(5):
            state[field, at] = west[WEST_FIELD[field] + at].astype(jnp.float32)
            state[field, HALO + COLS + at] = east[EAST_FIELD[field] + at].astype(jnp.float32)
        weight[at] = west[WEST_MASS + at].astype(jnp.float32)
        weight[HALO + COLS + at] = east[EAST_MASS + at].astype(jnp.float32)

    @pl.loop(0, STEPS)
    def _(step):
        for at in range(8):
            zeta[step, at] = west[west_slot(step) + at - step].astype(jnp.float32)
            zeta[step, HALO + COLS + at] = east[
                east_slot(step) + (EAST_WIDTH[0] - 1 - step) - at
            ].astype(jnp.float32)

    lane = lax.broadcasted_iota(jnp.int32, (8, LANES), 1)
    sub = lax.broadcasted_iota(jnp.int32, (8, LANES), 0)
    first_lane = lane == 0
    last_lane = lane == LANES - 1
    top = sub == 0
    bottom = sub == 7
    corner = last_lane & bottom

    def row_above(value):
        turned = pltpu.roll(value, LANES - 1, 1)
        even, odd = turned[:8], turned[8:]
        carried = jnp.where(bottom, 0.0, pltpu.roll(even, 7, 0))
        return jnp.concatenate([jnp.where(last_lane, odd, even), jnp.where(last_lane, carried, odd)], 0)

    def row_below(value):
        turned = pltpu.roll(value, 1, 1)
        even, odd = turned[:8], turned[8:]
        carried = jnp.where(top, 0.0, pltpu.roll(odd, 1, 0))
        return jnp.concatenate([jnp.where(first_lane, carried, even), jnp.where(first_lane, even, odd)], 0)

    def at_fold(value, add):
        return jnp.concatenate([value[:8], value[8:] + jnp.where(corner, add, 0.0)], 0)

    def forces(col):
        u, v, w = vel_u[col], vel_v[col], weight[col]
        wet = w != 0.0
        wet_u = jnp.where(wet, u, 0.0)
        wet_v = jnp.where(wet, v, 0.0)
        return w * u, w * v, wet_u - 0.1 * wet_v, wet_v + 0.1 * wet_u

    blank = jnp.zeros((TILE, LANES), jnp.float32)

    @pl.loop(0, STEPS)
    def _(step):
        begin = step
        groups = (2 * STEPS + COLS - 1 - 2 * step + UNROLL - 1) // UNROLL

        def body(group, carry):
            p, q, keep_u, keep_v, west_x, west_c = carry
            for part in range(UNROLL):
                col = begin + group * UNROLL + part
                next_p, next_q, next_u, next_v = forces(col + 1)
                along = 0.5 * (p - next_p)
                across = 0.5 * at_fold(row_below(q) - q, folds[8 + step, pl.ds(col, 1), :])
                turn = at_fold(row_below(p) - p, -folds[step, pl.ds(col, 1), :])
                new_one = one[col] + (along + across)
                new_two = two[col] + (along - across)
                new_shear = shear[col] + turn + (q - next_q)
                one[col] = new_one
                two[col] = new_two
                shear[col] = new_shear
                z = zeta[step, col]
                first = z * new_one
                quarter = 0.25 * z
                second = quarter * new_two
                c = quarter * new_shear
                x = first + second
                y = first - second
                vel_u[col] = keep_u + (west_x - x) + (c - row_above(c))
                vel_v[col] = keep_v + (west_c - c) + (y - row_above(y))
                p, q, keep_u, keep_v, west_x, west_c = next_p, next_q, next_u, next_v, x, c
            return p, q, keep_u, keep_v, west_x, west_c

        lax.fori_loop(0, groups, body, forces(begin) + (blank, blank))

    @pl.loop(0, 8)
    def _(at):
        for field in range(5):
            for half in range(2):
                tile = SHRINK * state[field, HALO + 8 * half + at]
                even, odd = column_slices(at, half)
                out[field, even, :] = tile[:8]
                out[field, odd, :] = tile[8:]


def on_device(final_cot, strains, strength, mass, ice_mask, partner):
    count = lax.axis_size("lon")
    state = as_rows(final_cot)
    whole = pl.BlockSpec(memory_space=pltpu.VMEM)
    hbm = pl.BlockSpec(memory_space=pltpu.HBM)
    f32 = jnp.float32
    bf16 = jnp.bfloat16
    params = pltpu.CompilerParams(vmem_limit_bytes=32 * 1024 * 1024)
    extended = (
        jax.ShapeDtypeStruct((5, EXT, TILE, LANES), f32),
        jax.ShapeDtypeStruct((STEPS, EXT, TILE, LANES), f32),
        jax.ShapeDtypeStruct((EXT, TILE, LANES), f32),
    )
    west_send, east_send, strip_send, state_ext, zeta_ext, mass_ext = pl.pallas_call(
        pack_kernel,
        out_shape=(
            jax.ShapeDtypeStruct((WEST_SIZE, TILE, LANES), bf16),
            jax.ShapeDtypeStruct((EAST_SIZE, TILE, LANES), bf16),
            jax.ShapeDtypeStruct((count, COLS, LANES), bf16),
            *extended,
        ),
        in_specs=[hbm] * 6,
        out_specs=(whole,) * 6,
        scratch_shapes=[
            pltpu.VMEM(state.shape, f32),
            pltpu.VMEM(strains.shape, bf16),
            pltpu.VMEM(strength.shape, f32),
            pltpu.VMEM(mass.shape, f32),
            pltpu.VMEM(ice_mask.shape, jnp.int32),
            pltpu.SMEM(partner.shape, jnp.int32),
            pltpu.VMEM((2, 256, LANES), f32),
            pltpu.SemaphoreType.DMA((5 + STEPS // 2,)),
        ],
        compiler_params=params,
    )(*(pltpu.with_memory_space_constraint(x, pltpu.HBM) for x in (state, strains, strength, mass, ice_mask, partner)))

    west = lax.ppermute(west_send, "lon", [(i, (i + 1) % count) for i in range(count)])
    east = lax.ppermute(east_send, "lon", [(i, (i - 1) % count) for i in range(count)])
    strips = lax.all_to_all(strip_send, "lon", 0, 0, tiled=True).reshape(count * COLS, LANES)

    out = pl.pallas_call(
        main_kernel,
        out_shape=(jax.ShapeDtypeStruct(state.shape, f32), *extended),
        in_specs=[whole] * 6,
        out_specs=(whole,) * 4,
        input_output_aliases={3: 1, 4: 2, 5: 3},
        scratch_shapes=[pltpu.VMEM((16, EXT, LANES), f32)],
        compiler_params=params,
    )(west, east, strips, state_ext, zeta_ext, mass_ext)
    return from_rows(out[0])


def solution(mesh):
    return jax.shard_map(
        on_device,
        mesh=mesh,
        in_specs=(
            P("ens", "lon", None),
            P("ens", None, "lon", None),
            P("lon", None),
            P("lon", None),
            P("lon", None),
            P("lon"),
        ),
        out_specs=P("ens", "lon", None),
        check_vma=False,
    )
```

```python
import functools

import jax
import jax.numpy as jnp
from jax import lax
from jax.experimental import pallas as pl
from jax.experimental.pallas import tpu as pltpu
from jax.sharding import PartitionSpec as P

COLS = 16
STEPS = 8
HALO = 8
TILE = 16
LANES = 128
GROUPS = 16
EXT = 40
UNROLL = 8

WEST_WIDTH = [STEPS + 1 - step for step in range(1, STEPS + 1)]
EAST_WIDTH = [STEPS - step for step in range(1, STEPS + 1)]
WEST_FIELD = [0, 8, 16, 24, 32]
WEST_COUNT = [8, 8, 8, 8, 8]
WEST_MASS = 40
WEST_ZETA = [48 + sum(WEST_WIDTH[:k]) for k in range(STEPS)]
WEST_SIZE = 48 + sum(WEST_WIDTH)
EAST_FIELD = [0, 8, 16, 23, 30]
EAST_COUNT = [8, 8, 7, 7, 7]
EAST_MASS = 37
EAST_ZETA = [45 + sum(EAST_WIDTH[:k]) for k in range(STEPS)]
EAST_SIZE = 45 + sum(EAST_WIDTH)
STRIP = 24
STRIP_FIELDS = 5
STRIP_PARTS = 3
EAST_END = EXT + 7
SHRINK = (5.0 / 6.0) ** STEPS


def as_rows(field):
    lead = field.shape[:-2]
    tiled = field.reshape(lead + (2, 8, GROUPS, LANES)).swapaxes(-3, -2)
    return tiled.reshape(lead + (2 * GROUPS * 8, LANES))


def from_rows(field):
    lead = field.shape[:-2]
    tiled = field.reshape(lead + (2, GROUPS, 8, LANES)).swapaxes(-3, -2)
    return tiled.reshape(lead + (COLS, GROUPS * LANES))


def column_slices(col, half):
    start = half * 128 + col
    return pl.ds(start, 8, 16), pl.ds(start + 8, 8, 16)


def column_tile(load, col, half):
    even, odd = column_slices(col, half)
    return jnp.concatenate([load(even), load(odd)], axis=0)


def west_slot(step):
    return 48 + STEPS * step - (step * (step - 1)) // 2


def east_slot(step):
    return 45 + (STEPS - 1) * step - (step * (step - 1)) // 2


def viscosity(rates, strength):
    square = rates[0] * rates[0] + 0.25 * (rates[1] * rates[1] + rates[2] * rates[2])
    return (0.1 * strength) * lax.rsqrt(jnp.maximum(square, 0.25))


def pack_kernel(
    state_hbm, strains_hbm, strength_hbm, mass_hbm, mask_hbm, partner_hbm,
    west_out, east_out, strip_out, own_out, state_out, zeta_out, mass_out,
    state, strains, strength, mass, mask, partner, rows, top, sems,
):
    bf16 = jnp.bfloat16
    cell_copies = [
        pltpu.make_async_copy(mass_hbm, mass, sems.at[0]),
        pltpu.make_async_copy(mask_hbm, mask, sems.at[1]),
    ]
    state_copy = pltpu.make_async_copy(state_hbm, state, sems.at[2])
    late_copies = [
        pltpu.make_async_copy(strength_hbm, strength, sems.at[3]),
        pltpu.make_async_copy(partner_hbm, partner, sems.at[4]),
    ]
    strain_copies = [
        pltpu.make_async_copy(strains_hbm.at[2 * k : 2 * k + 2], strains.at[2 * k : 2 * k + 2], sems.at[5 + k])
        for k in range(STEPS // 2)
    ]
    for copy in [*cell_copies, state_copy, *late_copies, *strain_copies]:
        copy.start()

    for copy in cell_copies:
        copy.wait()
    for group in range(GROUPS):
        at = slice(LANES * group, LANES * group + LANES)
        weight = mask[:, at].astype(jnp.float32) / (6.0 * mass[:, at])
        rows[0, 8 * group : 8 * group + 8] = weight[:8]
        rows[0, 128 + 8 * group : 136 + 8 * group] = weight[8:]
    top[5] = weight
    for at in range(8):
        tile = column_tile(lambda part: rows[0, part, :], at, 0)
        mass_out[HALO + at] = tile
        east_out[EAST_MASS + at] = tile.astype(bf16)
        tile = column_tile(lambda part: rows[0, part, :], at, 1)
        mass_out[HALO + 8 + at] = tile
        west_out[WEST_MASS + at] = tile.astype(bf16)
    spared = mass_out[HALO + 7].astype(bf16)
    east_first = mass_out[HALO].astype(bf16)

    state_copy.wait()

    @pl.loop(0, 8)
    def _(turn):
        at = 7 - turn
        for field in range(5):
            tile = column_tile(lambda part: state[field, part, :], at, 0)
            state_out[field, HALO + at] = tile
            east_out[EAST_FIELD[field] + at] = tile.astype(bf16)
            tile = column_tile(lambda part: state[field, part, :], at, 1)
            state_out[field, HALO + 8 + at] = tile
            west_out[WEST_FIELD[field] + at] = tile.astype(bf16)

    for field in range(5):
        top[field, :8] = state[field, 120:128, :]
        top[field, 8:] = state[field, 248:256, :]
    for copy in late_copies:
        copy.wait()

    def cycle_zeta(cycle, step, rows):
        for group in range(GROUPS):
            at = slice(LANES * group, LANES * group + LANES)
            rates = [strains[cycle, k, :, at].astype(jnp.float32) for k in range(3)]
            zeta = viscosity(rates, strength[:, at])
            rows[8 * group : 8 * group + 8] = zeta[:8]
            rows[128 + 8 * group : 136 + 8 * group] = zeta[8:]
        top[6 + step] = zeta
        for at in range(8):
            tile = column_tile(lambda part: rows[part, :], at, 0)
            zeta_out[step, HALO + at] = tile
            east_out[east_slot(step) + (EAST_WIDTH[0] - 1 - step) - at] = tile.astype(bf16)
            tile = column_tile(lambda part: rows[part, :], at, 1)
            zeta_out[step, HALO + 8 + at] = tile
            west_out[west_slot(step) + at - step] = tile.astype(bf16)

    @pl.loop(0, STEPS // 2)
    def _(turn):
        pltpu.make_async_copy(
            strains_hbm.at[pl.ds(2 * turn, 2)], strains.at[pl.ds(2 * turn, 2)], sems.at[5 + turn]
        ).wait()
        for part in range(2):
            cycle = 2 * turn + part
            cycle_zeta(cycle, STEPS - 1 - cycle, rows.at[part])

    east_out[EAST_MASS] = east_first
    east_out[EAST_MASS + 7] = spared

    lane = lax.broadcasted_iota(jnp.int32, (COLS, LANES), 1)
    row_at = lax.broadcasted_iota(jnp.int32, (COLS, LANES), 0)
    place = jnp.zeros((COLS, LANES), jnp.int32)
    for col in range(COLS):
        place = jnp.where(row_at == col, lax.rem(partner[col], COLS), place)
    strips = [place.astype(jnp.float32)] + [jnp.zeros((COLS, LANES), jnp.float32)] * (STRIP_PARTS - 1)
    for at in range(6 + STEPS):
        part, begin = at // STRIP_FIELDS, STRIP * (at % STRIP_FIELDS)
        moved = pltpu.roll(top[at], (begin + STRIP) % LANES, 1)
        strips[part] = jnp.where((lane >= begin) & (lane < begin + STRIP), moved, strips[part])
    for part in range(STRIP_PARTS):
        own_out[0, part] = strips[part]
        strip_out[0, part] = strips[part].astype(bf16)


def join_kernel(count, *refs):
    out = refs[(len(refs) + count - 1) // 2]
    at = 0
    for part in refs[:count]:
        size = part.shape[0]
        out[at : at + size] = part[...]
        at += size


def fold_kernel(offsets, *refs):
    *parts, own, last_tiles, _, out, strips, tiles, sems = refs
    me = lax.axis_index("lon")
    blocks = strips.shape[0]
    total = blocks * COLS
    count = total // LANES
    order = iter(offsets)
    for part in parts:
        for k in range(part.shape[0]):
            strips[next(order)] = part[k].astype(jnp.float32)
    strips[0] = own[0]
    lane = lax.broadcasted_iota(jnp.int32, (STRIP, LANES), 1)
    sub = lax.broadcasted_iota(jnp.int32, (STRIP, total), 0)
    last = sub == STRIP - 1
    turned = [
        [
            jnp.concatenate([strips[lax.bitwise_xor(me, 8 * r + k), part] for k in range(8)], axis=0).T
            for r in range(count)
        ]
        for part in range(STRIP_PARTS)
    ]

    def field(at):
        part, begin = at // STRIP_FIELDS, STRIP * (at % STRIP_FIELDS)
        return jnp.concatenate([tile[begin : begin + STRIP] for tile in turned[part]], axis=1)

    begin = STRIP * STRIP_FIELDS
    places = [
        (7 - lane[:8] // COLS) * COLS + jnp.broadcast_to(tile[begin : begin + 1], (8, LANES)).astype(jnp.int32)
        for tile in turned[0]
    ]

    def at_fold(value):
        rows = [
            jnp.take_along_axis(
                value[STRIP - 8 :, LANES * (count - 1 - r) : LANES * (count - r)], places[r], axis=1,
                mode="promise_in_bounds",
            )
            for r in range(count)
        ]
        far = jnp.where(last[:8] | last[STRIP - 8 :], jnp.concatenate(rows, axis=1), 0.0)
        return jnp.concatenate([jnp.zeros((STRIP - 8, total), jnp.float32), far], axis=0)

    def next_col(value):
        return pltpu.roll(value, total - 1, 1)

    def prev_col(value):
        return pltpu.roll(value, 1, 1)

    def row_above(value):
        return jnp.where(last, 0.0, pltpu.roll(value, STRIP - 1, 0))

    def row_below(value):
        return pltpu.roll(value, 1, 0)

    vel_u, vel_v, one, two, shear, weight = (field(at) for at in range(6))
    wet = weight != 0.0
    for step in range(STEPS):
        p = weight * vel_u
        q = weight * vel_v
        along = 0.5 * (p - next_col(p))
        across = 0.5 * (row_below(q) - q + at_fold(q))
        one = one + (along + across)
        two = two + (along - across)
        shear = shear + (row_below(p) - p - at_fold(p)) + (q - next_col(q))
        zeta = field(6 + step)
        first = zeta * one
        quarter = 0.25 * zeta
        second = quarter * two
        third = quarter * shear
        x = first + second
        y = first - second
        wet_u = jnp.where(wet, vel_u, 0.0)
        wet_v = jnp.where(wet, vel_v, 0.0)
        vel_u = (wet_u - 0.1 * wet_v) + (prev_col(x) - x) + (third - row_above(third))
        vel_v = (wet_v + 0.1 * wet_u) + (prev_col(third) - third) + (y - row_above(y))

    shift = lax.rem(total - COLS * me, total)
    rows = [pltpu.roll(value, shift, 1)[:, :LANES] for value in (vel_u, vel_v, one, two, shear)]
    rows.append(jnp.zeros((LANES - STRIP * STRIP_FIELDS, LANES), jnp.float32))
    top = SHRINK * jnp.concatenate(rows, axis=0).T[:COLS]
    reached = lane[:COLS] >= LANES - STEPS - 1
    for field in range(5):
        moved = pltpu.roll(top, (LANES - STRIP - STRIP * field) % LANES, 1)
        tiles[field] = jnp.where(reached, moved, last_tiles[field])
    copies = [
        pltpu.make_async_copy(tiles.at[:, 8 * half : 8 * half + 8, :], out.at[:, pl.ds(128 * half + 120, 8), :], sems.at[half])
        for half in range(2)
    ]
    for copy in copies:
        copy.start()
    for copy in copies:
        copy.wait()


def stepper(state, zeta, weight):
    vel_u, vel_v, one, two, shear = (state.at[field] for field in range(5))
    lane = lax.broadcasted_iota(jnp.int32, (8, LANES), 1)
    sub = lax.broadcasted_iota(jnp.int32, (8, LANES), 0)
    first_lane = lane == 0
    last_lane = lane == LANES - 1
    top = sub == 0
    bottom = sub == 7

    def row_above(value):
        turned = pltpu.roll(value, LANES - 1, 1)
        even, odd = turned[:8], turned[8:]
        carried = jnp.where(bottom, 0.0, pltpu.roll(even, 7, 0))
        return jnp.concatenate([jnp.where(last_lane, odd, even), jnp.where(last_lane, carried, odd)], 0)

    def row_below(value):
        turned = pltpu.roll(value, 1, 1)
        even, odd = turned[:8], turned[8:]
        carried = jnp.where(top, 0.0, pltpu.roll(odd, 1, 0))
        return jnp.concatenate([jnp.where(first_lane, carried, even), jnp.where(first_lane, even, odd)], 0)

    def forces(place, col):
        u, v, w = vel_u[place], vel_v[place], weight[col]
        wet = w != 0.0
        wet_u = jnp.where(wet, u, 0.0)
        wet_v = jnp.where(wet, v, 0.0)
        return w * u, w * v, wet_u - 0.1 * wet_v, wet_v + 0.1 * wet_u

    def strains_of(step, col, one_at, two_at, shear_at):
        z = zeta[step, col]
        first = z * one_at
        quarter = 0.25 * z
        second = quarter * two_at
        return first + second, quarter * shear_at, first - second

    def stored_strains(step, place, col):
        return strains_of(step, col, one[place], two[place], shear[place])

    def velocities(keep_u, keep_v, west_x, west_c, x, c, y):
        return keep_u + (west_x - x) + (c - row_above(c)), keep_v + (west_c - c) + (y - row_above(y))

    def advance(step, place, next_place, col, carry):
        p, q, keep_u, keep_v, west_x, west_c = carry
        next_p, next_q, next_u, next_v = forces(next_place, col + 1)
        along = 0.5 * (p - next_p)
        across = 0.5 * (row_below(q) - q)
        turn = row_below(p) - p
        new_one = one[place] + (along + across)
        new_two = two[place] + (along - across)
        new_shear = shear[place] + turn + (q - next_q)
        x, c, y = strains_of(step, col, new_one, new_two, new_shear)
        new_u, new_v = velocities(keep_u, keep_v, west_x, west_c, x, c, y)
        return (new_u, new_v, new_one, new_two, new_shear), (next_p, next_q, next_u, next_v, x, c)

    return forces, stored_strains, velocities, advance


def inner_kernel(state_in, zeta, weight, sides, state):
    forces, _, _, advance = stepper(state, zeta, weight)
    blank = jnp.zeros((TILE, LANES), jnp.float32)

    @pl.loop(0, STEPS)
    def _(step):
        begin = HALO + step
        last = HALO + COLS - 2 - step

        def body(group, carry):
            for part in range(UNROLL):
                col = begin + group * UNROLL + part
                new, carry = advance(step, col, col + 1, col, carry)
                for field in range(5):
                    valid = (col <= last) & (col > begin) if field < 2 else col <= last
                    state[field, col] = jnp.where(valid, new[field], state[field, col])
            return carry

        lax.fori_loop(0, (last - begin + UNROLL) // UNROLL, body, forces(begin, begin) + (blank, blank))

    @pl.loop(0, 9)
    def _(at):
        for field in range(5):
            sides[field, HALO + at] = state[field, HALO + at]
            sides[field, EAST_END - HALO - 7 - at] = state[field, HALO + 7 + at]


def edge_kernel(west, east, state_in, zeta_in, mass_in, out, last, state, zeta, weight):
    @pl.loop(0, 8)
    def _(at):
        for field in range(5):
            state[field, at] = west[WEST_FIELD[field] + at].astype(jnp.float32)
            state[field, EAST_END - HALO - COLS - at] = east[EAST_FIELD[field] + at].astype(jnp.float32)
        weight[at] = west[WEST_MASS + at].astype(jnp.float32)
        weight[HALO + COLS + at] = east[EAST_MASS + at].astype(jnp.float32)

    @pl.loop(0, STEPS)
    def _(step):
        for at in range(8):
            zeta[step, at] = west[west_slot(step) + at - step].astype(jnp.float32)
            zeta[step, HALO + COLS + at] = east[
                east_slot(step) + (EAST_WIDTH[0] - 1 - step) - at
            ].astype(jnp.float32)

    forces, stored_strains, velocities, advance = stepper(state, zeta, weight)
    blank = jnp.zeros((TILE, LANES), jnp.float32)

    start = EAST_END - (HALO + COLS - 1)

    @pl.loop(0, STEPS)
    def _(step):
        begin = HALO + COLS - 1 - step
        x, c, _ = stored_strains(step, step + (start + 1), begin - 1)
        carry = forces(step + start, begin) + (x, c)
        west_carry = forces(step, step) + (blank, blank)
        for part in range(8):
            new, carry = advance(step, step + (start - part), step + (start - part - 1), begin + part, carry)
            west_new, west_carry = advance(step, step + part, step + part + 1, step + part, west_carry)
            for field in range(5):
                state[field, step + (start - part)] = new[field]
                state[field, step + part] = west_new[field]
        u, v = velocities(*west_carry[2:], *stored_strains(step, step + 8, step + 8))
        state[0, step + 8] = u
        state[1, step + 8] = v

    @pl.loop(0, 8)
    def _(at):
        for field in range(5):
            for half in range(2):
                tile = SHRINK * state[field, (HALO + at, EAST_END - HALO - 8 - at)[half]]
                even, odd = column_slices(at, half)
                out[field, even, :] = tile[:8]
                out[field, odd, :] = tile[8:]

    for field in range(5):
        last[field, :8] = out[field, 120:128, :]
        last[field, 8:] = out[field, 248:256, :]


def join(parts, passed):
    whole = pl.BlockSpec(memory_space=pltpu.VMEM)
    size = sum(part.shape[0] for part in parts)
    held, *passed = pl.pallas_call(
        functools.partial(join_kernel, len(parts)),
        out_shape=(
            jax.ShapeDtypeStruct((size, *parts[0].shape[1:]), parts[0].dtype),
            *(jax.ShapeDtypeStruct(x.shape, x.dtype) for x in passed),
        ),
        in_specs=[whole] * (len(parts) + len(passed)),
        out_specs=(whole,) * (1 + len(passed)),
        input_output_aliases={len(parts) + k: 1 + k for k in range(len(passed))},
        compiler_params=pltpu.CompilerParams(vmem_limit_bytes=16 * 1024 * 1024),
    )(*parts, *passed)
    return held, passed


def gather_stages(count):
    stages = []
    bit = 4
    while bit < count:
        stages.append((bit, 2 * bit, 3 * bit) if 2 * bit < count else (bit,))
        bit *= 4
    return stages + [(1,), (2,)]


def exchange(held, steps, count):
    return [held] + [lax.ppermute(held, "lon", [(i, i ^ step) for i in range(count)]) for step in steps]


def on_device(final_cot, strains, strength, mass, ice_mask, partner):
    count = lax.axis_size("lon")
    whole = pl.BlockSpec(memory_space=pltpu.VMEM)
    hbm = pl.BlockSpec(memory_space=pltpu.HBM)
    f32 = jnp.float32
    bf16 = jnp.bfloat16
    params = pltpu.CompilerParams(vmem_limit_bytes=16 * 1024 * 1024)
    cells = [
        pltpu.with_memory_space_constraint(x, pltpu.HBM)
        for x in (as_rows(final_cot), strains, strength, mass, ice_mask, partner)
    ]
    state_shape = cells[0].shape
    extended = (
        jax.ShapeDtypeStruct((5, EXT, TILE, LANES), f32),
        jax.ShapeDtypeStruct((STEPS, EXT, TILE, LANES), f32),
        jax.ShapeDtypeStruct((EXT, TILE, LANES), f32),
    )
    sends = (
        jax.ShapeDtypeStruct((WEST_SIZE, TILE, LANES), bf16),
        jax.ShapeDtypeStruct((EAST_SIZE, TILE, LANES), bf16),
    )
    west_send, east_send, strip, own_strip, state, zeta, weight = pl.pallas_call(
        pack_kernel,
        out_shape=(
            *sends,
            jax.ShapeDtypeStruct((1, STRIP_PARTS, COLS, LANES), bf16),
            jax.ShapeDtypeStruct((1, STRIP_PARTS, COLS, LANES), f32),
            *extended,
        ),
        in_specs=[hbm] * 6,
        out_specs=(whole,) * 7,
        scratch_shapes=[
            pltpu.VMEM(state_shape, f32),
            pltpu.VMEM(strains.shape, bf16),
            pltpu.VMEM(strength.shape, f32),
            pltpu.VMEM(mass.shape, f32),
            pltpu.VMEM(ice_mask.shape, jnp.int32),
            pltpu.SMEM(partner.shape, jnp.int32),
            pltpu.VMEM((2, 256, LANES), f32),
            pltpu.VMEM((6 + STEPS, COLS, LANES), f32),
            pltpu.SemaphoreType.DMA((5 + STEPS // 2,)),
        ],
        compiler_params=params,
    )(*cells)
    west = lax.ppermute(west_send, "lon", [(i, (i + 1) % count) for i in range(count)])
    east = lax.ppermute(east_send, "lon", [(i, (i - 1) % count) for i in range(count)])
    state, _ = pl.pallas_call(
        inner_kernel,
        out_shape=(extended[0], extended[0]),
        in_specs=[whole] * 3,
        out_specs=(whole,) * 2,
        input_output_aliases={0: 1},
        compiler_params=params,
    )(state, zeta, weight)
    offsets = [0]
    parts = [strip]
    for steps in gather_stages(count):
        held = parts[0]
        if len(parts) > 1:
            held, (state,) = join(parts, (state,))
        parts = exchange(held, steps, count)
        offsets = [offset ^ step for step in (0, *steps) for offset in offsets]
    out, last, *_ = pl.pallas_call(
        edge_kernel,
        out_shape=(
            jax.ShapeDtypeStruct(state_shape, f32),
            jax.ShapeDtypeStruct((5, COLS, LANES), f32),
            *extended,
        ),
        in_specs=[whole] * 5,
        out_specs=(whole,) * 5,
        input_output_aliases={2: 2, 3: 3, 4: 4},
        compiler_params=params,
    )(west, east, state, zeta, weight)
    out = pl.pallas_call(
        functools.partial(fold_kernel, offsets),
        out_shape=jax.ShapeDtypeStruct(state_shape, f32),
        in_specs=[whole] * (len(parts) + 2) + [hbm],
        out_specs=hbm,
        input_output_aliases={len(parts) + 2: 0},
        scratch_shapes=[
            pltpu.VMEM((count, STRIP_PARTS, COLS, LANES), f32),
            pltpu.VMEM((5, COLS, LANES), f32),
            pltpu.SemaphoreType.DMA((2,)),
        ],
        compiler_params=params,
    )(*parts, own_strip, last, pltpu.with_memory_space_constraint(out, pltpu.HBM))
    return from_rows(out)


def solution(mesh):
    return jax.shard_map(
        on_device,
        mesh=mesh,
        in_specs=(
            P("ens", "lon", None),
            P("ens", None, "lon", None),
            P("lon", None),
            P("lon", None),
            P("lon", None),
            P("lon"),
        ),
        out_specs=P("ens", "lon", None),
        check_vma=False,
    )
```

```python
import functools

import jax
import jax.numpy as jnp
from jax import lax
from jax.experimental import pallas as pl
from jax.experimental.pallas import tpu as pltpu
from jax.sharding import PartitionSpec as P

COLS = 16
STEPS = 8
HALO = 8
TILE = 16
LANES = 128
GROUPS = 16
EXT = 40
UNROLL = 8

WEST_COLS = [4, 5, 6, 7]
EAST_COLS = [24, 25, 26, 27]


def numbered(entries):
    return {entry: at for at, entry in enumerate(entries)}


WEST_PLACES = numbered(
    [("state", field, col) for field in range(5) for col in WEST_COLS]
    + [("state", field, 3) for field in range(2, 5)]
    + [("mass", 0, col) for col in WEST_COLS]
    + [
        ("zeta", step, col)
        for step in range(STEPS)
        for col in range(6 - step if step < 4 else step, 8)
    ]
)
EAST_PLACES = numbered(
    [("state", field, col) for field in range(5) for col in EAST_COLS]
    + [("mass", 0, col) for col in EAST_COLS]
    + [
        ("zeta", step, col)
        for step in range(STEPS)
        for col in range(24, 25 + step if step < 4 else 31 - step)
    ]
)
WEST_SIZE = len(WEST_PLACES)
EAST_SIZE = len(EAST_PLACES)
STRIP = 24
STRIP_FIELDS = 5
STRIP_PARTS = 3
EAST_END = EXT + 7
EDGE_SPLIT = 4
SHRINK = (5.0 / 6.0) ** STEPS


def as_rows(field):
    lead = field.shape[:-2]
    tiled = field.reshape(lead + (2, 8, GROUPS, LANES)).swapaxes(-3, -2)
    return tiled.reshape(lead + (2 * GROUPS * 8, LANES))


def from_rows(field):
    lead = field.shape[:-2]
    tiled = field.reshape(lead + (2, GROUPS, 8, LANES)).swapaxes(-3, -2)
    return tiled.reshape(lead + (COLS, GROUPS * LANES))


def column_slices(col, half):
    start = half * 128 + col
    return pl.ds(start, 8, 16), pl.ds(start + 8, 8, 16)


def column_tile(load, col, half):
    even, odd = column_slices(col, half)
    return jnp.concatenate([load(even), load(odd)], axis=0)


def viscosity(rates, strength):
    square = rates[0] * rates[0] + 0.25 * (rates[1] * rates[1] + rates[2] * rates[2])
    return (0.1 * strength) * lax.rsqrt(jnp.maximum(square, 0.25))


def pack_kernel(
    state_hbm, strains_hbm, strength_hbm, mass_hbm, mask_hbm, partner_hbm,
    strip_out, own_out, state_out, zeta_out, mass_out,
    state, strains, strength, mass, mask, partner, rows, top, sems,
):
    bf16 = jnp.bfloat16
    cell_copies = [
        pltpu.make_async_copy(mass_hbm, mass, sems.at[0]),
        pltpu.make_async_copy(mask_hbm, mask, sems.at[1]),
    ]
    state_copy = pltpu.make_async_copy(state_hbm, state, sems.at[2])
    late_copies = [
        pltpu.make_async_copy(strength_hbm, strength, sems.at[3]),
        pltpu.make_async_copy(partner_hbm, partner, sems.at[4]),
    ]
    strain_copies = [
        pltpu.make_async_copy(strains_hbm.at[2 * k : 2 * k + 2], strains.at[2 * k : 2 * k + 2], sems.at[5 + k])
        for k in range(STEPS // 2)
    ]
    for copy in [*cell_copies, state_copy, *late_copies, *strain_copies]:
        copy.start()

    for copy in cell_copies:
        copy.wait()
    for group in range(GROUPS):
        at = slice(LANES * group, LANES * group + LANES)
        weight = mask[:, at].astype(jnp.float32) / (6.0 * mass[:, at])
        rows[0, 8 * group : 8 * group + 8] = weight[:8]
        rows[0, 128 + 8 * group : 136 + 8 * group] = weight[8:]
    top[5] = weight
    for at in range(8):
        tile = column_tile(lambda part: rows[0, part, :], at, 0)
        mass_out[HALO + at] = tile
        tile = column_tile(lambda part: rows[0, part, :], at, 1)
        mass_out[HALO + 8 + at] = tile
    state_copy.wait()

    @pl.loop(0, 8)
    def _(at):
        for field in range(5):
            state_out[field, HALO + at] = column_tile(lambda part: state[field, part, :], at, 0)
            state_out[field, HALO + 8 + at] = column_tile(lambda part: state[field, part, :], at, 1)

    for field in range(5):
        top[field, :8] = state[field, 120:128, :]
        top[field, 8:] = state[field, 248:256, :]
    for copy in late_copies:
        copy.wait()

    def cycle_zeta(cycle, step, rows):
        for group in range(GROUPS):
            at = slice(LANES * group, LANES * group + LANES)
            rates = [strains[cycle, k, :, at].astype(jnp.float32) for k in range(3)]
            zeta = viscosity(rates, strength[:, at])
            rows[8 * group : 8 * group + 8] = zeta[:8]
            rows[128 + 8 * group : 136 + 8 * group] = zeta[8:]
        top[6 + step] = zeta
        for at in range(8):
            zeta_out[step, HALO + at] = column_tile(lambda part: rows[part, :], at, 0)
            zeta_out[step, HALO + 8 + at] = column_tile(lambda part: rows[part, :], at, 1)

    @pl.loop(0, STEPS // 2)
    def _(turn):
        pltpu.make_async_copy(
            strains_hbm.at[pl.ds(2 * turn, 2)], strains.at[pl.ds(2 * turn, 2)], sems.at[5 + turn]
        ).wait()
        for part in range(2):
            cycle = 2 * turn + part
            cycle_zeta(cycle, STEPS - 1 - cycle, rows.at[part])

    lane = lax.broadcasted_iota(jnp.int32, (COLS, LANES), 1)
    row_at = lax.broadcasted_iota(jnp.int32, (COLS, LANES), 0)
    place = jnp.zeros((COLS, LANES), jnp.int32)
    for col in range(COLS):
        place = jnp.where(row_at == col, lax.rem(partner[col], COLS), place)
    strips = [place.astype(jnp.float32)] + [jnp.zeros((COLS, LANES), jnp.float32)] * (STRIP_PARTS - 1)
    for at in range(6 + STEPS):
        part, begin = at // STRIP_FIELDS, STRIP * (at % STRIP_FIELDS)
        moved = pltpu.roll(top[at], (begin + STRIP) % LANES, 1)
        strips[part] = jnp.where((lane >= begin) & (lane < begin + STRIP), moved, strips[part])
    for part in range(STRIP_PARTS):
        own_out[0, part] = strips[part]
        strip_out[0, part] = strips[part].astype(bf16)


def join_kernel(count, *refs):
    out = refs[(len(refs) + count - 1) // 2]
    at = 0
    for part in refs[:count]:
        size = part.shape[0]
        out[at : at + size] = part[...]
        at += size


def fold_kernel(offsets, *refs):
    *parts, own, result, out, strips, tiles, sems = refs
    copies = [
        pltpu.make_async_copy(result.at[:, pl.ds(at, 120), :], out.at[:, pl.ds(at, 120), :], sems.at[at // 128])
        for at in (0, 128)
    ]
    for copy in copies:
        copy.start()
    me = lax.axis_index("lon")
    blocks = strips.shape[0]
    total = blocks * COLS
    count = total // LANES
    order = iter(offsets)
    for part in parts:
        for k in range(part.shape[0]):
            strips[next(order)] = part[k].astype(jnp.float32)
    strips[0] = own[0]
    lane = lax.broadcasted_iota(jnp.int32, (STRIP, LANES), 1)
    sub = lax.broadcasted_iota(jnp.int32, (STRIP, total), 0)
    last = sub == STRIP - 1
    turned = [
        [
            jnp.concatenate([strips[lax.bitwise_xor(me, 8 * r + k), part] for k in range(8)], axis=0).T
            for r in range(count)
        ]
        for part in range(STRIP_PARTS)
    ]

    def field(at):
        part, begin = at // STRIP_FIELDS, STRIP * (at % STRIP_FIELDS)
        return jnp.concatenate([tile[begin : begin + STRIP] for tile in turned[part]], axis=1)

    begin = STRIP * STRIP_FIELDS
    places = [
        (7 - lane[:8] // COLS) * COLS + jnp.broadcast_to(tile[begin : begin + 1], (8, LANES)).astype(jnp.int32)
        for tile in turned[0]
    ]

    def at_fold(value):
        rows = [
            jnp.take_along_axis(
                value[STRIP - 8 :, LANES * (count - 1 - r) : LANES * (count - r)], places[r], axis=1,
                mode="promise_in_bounds",
            )
            for r in range(count)
        ]
        far = jnp.where(last[:8] | last[STRIP - 8 :], jnp.concatenate(rows, axis=1), 0.0)
        return jnp.concatenate([jnp.zeros((STRIP - 8, total), jnp.float32), far], axis=0)

    def next_col(value):
        return pltpu.roll(value, total - 1, 1)

    def prev_col(value):
        return pltpu.roll(value, 1, 1)

    def row_above(value):
        return jnp.where(last, 0.0, pltpu.roll(value, STRIP - 1, 0))

    def row_below(value):
        return pltpu.roll(value, 1, 0)

    vel_u, vel_v, one, two, shear, weight = (field(at) for at in range(6))
    wet = weight != 0.0
    for step in range(STEPS):
        p = weight * vel_u
        q = weight * vel_v
        along = 0.5 * (p - next_col(p))
        across = 0.5 * (row_below(q) - q + at_fold(q))
        one = one + (along + across)
        two = two + (along - across)
        shear = shear + (row_below(p) - p - at_fold(p)) + (q - next_col(q))
        zeta = field(6 + step)
        first = zeta * one
        quarter = 0.25 * zeta
        second = quarter * two
        third = quarter * shear
        x = first + second
        y = first - second
        wet_u = jnp.where(wet, vel_u, 0.0)
        wet_v = jnp.where(wet, vel_v, 0.0)
        vel_u = (wet_u - 0.1 * wet_v) + (prev_col(x) - x) + (third - row_above(third))
        vel_v = (wet_v + 0.1 * wet_u) + (prev_col(third) - third) + (y - row_above(y))

    shift = lax.rem(total - COLS * me, total)
    rows = [pltpu.roll(value, shift, 1)[:, :LANES] for value in (vel_u, vel_v, one, two, shear)]
    rows.append(jnp.zeros((LANES - STRIP * STRIP_FIELDS, LANES), jnp.float32))
    top = SHRINK * jnp.concatenate(rows, axis=0).T[:COLS]
    reached = lane[:COLS] >= LANES - STEPS - 1
    for field in range(5):
        moved = pltpu.roll(top, (LANES - STRIP - STRIP * field) % LANES, 1)
        before = jnp.concatenate([result[field, 120:128, :], result[field, 248:256, :]], axis=0)
        tiles[field] = jnp.where(reached, moved, before)
    last_copies = [
        pltpu.make_async_copy(
            tiles.at[:, 8 * half : 8 * half + 8, :], out.at[:, pl.ds(128 * half + 120, 8), :], sems.at[2 + half]
        )
        for half in range(2)
    ]
    for copy in last_copies:
        copy.start()
    copies.extend(last_copies)
    for copy in copies:
        copy.wait()


def stepper(state, zeta, weight):
    vel_u, vel_v, one, two, shear = (state.at[field] for field in range(5))
    lane = lax.broadcasted_iota(jnp.int32, (8, LANES), 1)
    sub = lax.broadcasted_iota(jnp.int32, (8, LANES), 0)
    first_lane = lane == 0
    last_lane = lane == LANES - 1
    top = sub == 0
    bottom = sub == 7

    def row_above(value):
        turned = pltpu.roll(value, LANES - 1, 1)
        even, odd = turned[:8], turned[8:]
        carried = jnp.where(bottom, 0.0, pltpu.roll(even, 7, 0))
        return jnp.concatenate([jnp.where(last_lane, odd, even), jnp.where(last_lane, carried, odd)], 0)

    def row_below(value):
        turned = pltpu.roll(value, 1, 1)
        even, odd = turned[:8], turned[8:]
        carried = jnp.where(top, 0.0, pltpu.roll(odd, 1, 0))
        return jnp.concatenate([jnp.where(first_lane, carried, even), jnp.where(first_lane, even, odd)], 0)

    def forces(place, col):
        u, v, w = vel_u[place], vel_v[place], weight[col]
        wet = w != 0.0
        wet_u = jnp.where(wet, u, 0.0)
        wet_v = jnp.where(wet, v, 0.0)
        return w * u, w * v, wet_u - 0.1 * wet_v, wet_v + 0.1 * wet_u

    def strains_of(step, col, one_at, two_at, shear_at):
        z = zeta[step, col]
        first = z * one_at
        quarter = 0.25 * z
        second = quarter * two_at
        return first + second, quarter * shear_at, first - second

    def stored_strains(step, place, col):
        return strains_of(step, col, one[place], two[place], shear[place])

    def velocities(keep_u, keep_v, west_x, west_c, x, c, y):
        return keep_u + (west_x - x) + (c - row_above(c)), keep_v + (west_c - c) + (y - row_above(y))

    def advance(step, place, next_place, col, carry, moves=None):
        p, q, keep_u, keep_v, west_x, west_c = carry
        next_p, next_q, next_u, next_v = forces(next_place, col + 1)
        along = 0.5 * (p - next_p)
        across = 0.5 * (row_below(q) - q)
        turn = row_below(p) - p
        new_one = one[place] + (along + across)
        new_two = two[place] + (along - across)
        new_shear = shear[place] + turn + (q - next_q)
        if moves is not None:
            new_one = jnp.where(moves, new_one, one[place])
            new_two = jnp.where(moves, new_two, two[place])
            new_shear = jnp.where(moves, new_shear, shear[place])
        x, c, y = strains_of(step, col, new_one, new_two, new_shear)
        new_u, new_v = velocities(keep_u, keep_v, west_x, west_c, x, c, y)
        return (new_u, new_v, new_one, new_two, new_shear), (next_p, next_q, next_u, next_v, x, c)

    return forces, stored_strains, velocities, advance


def inner_steps(state, zeta, weight, steps, width):
    forces, _, _, advance = stepper(state, zeta, weight)
    blank = jnp.zeros((TILE, LANES), jnp.float32)

    @pl.loop(*steps)
    def _(step):
        begin = HALO + step
        last = HALO + COLS - 2 - step
        carry = forces(begin, begin) + (blank, blank)
        for part in range(width):
            col = begin + part
            new, carry = advance(step, col, col + 1, col, carry)
            for field in range(5):
                valid = (col <= last) & (part > 0) if field < 2 else col <= last
                state[field, col] = jnp.where(valid, new[field], state[field, col])


def first_inner_kernel(state_in, zeta, weight, state, west, east):
    inner_steps(state, zeta, weight, (0, EDGE_SPLIT), COLS - 1)
    for out, places, shift in ((west, WEST_PLACES, COLS), (east, EAST_PLACES, -COLS)):
        for (kind, which, col), place in places.items():
            source = {"state": state, "zeta": zeta}[kind].at[which] if kind != "mass" else weight
            out[place] = source[col + shift].astype(jnp.bfloat16)


def second_inner_kernel(state_in, zeta, weight, sides, state):
    inner_steps(state, zeta, weight, (EDGE_SPLIT, STEPS), COLS - 1 - 2 * EDGE_SPLIT)

    @pl.loop(0, 9)
    def _(at):
        for field in range(5):
            sides[field, HALO + at] = state[field, HALO + at]
            sides[field, EAST_END - HALO - 7 - at] = state[field, HALO + 7 + at]


def edge_kernel(west, east, state_in, zeta_in, mass_in, out, state, zeta, weight):
    for source, places in ((west, WEST_PLACES), (east, EAST_PLACES)):
        for (kind, which, col), place in places.items():
            tile = source[place].astype(jnp.float32)
            if kind == "state":
                state[which, EAST_END - col if col >= HALO + COLS else col] = tile
            elif kind == "mass":
                weight[col] = tile
            else:
                zeta[which, col] = tile

    forces, stored_strains, velocities, advance = stepper(state, zeta, weight)
    blank = jnp.zeros((TILE, LANES), jnp.float32)

    def growing(steps, reach):
        @pl.loop(*steps)
        def _(step):
            for middle in (HALO - 1, HALO + COLS - 1):
                cols = range(middle - reach, middle + reach + 2)
                at = [col if middle < HALO else EAST_END - col for col in range(cols[0], cols[-1] + 2)]
                carry = forces(at[0], cols[0]) + (blank, blank)
                for part, col in enumerate(cols):
                    old = [state[field, at[part]] for field in range(5)]
                    left = abs(col - middle) <= step
                    new, carry = advance(step, at[part], at[part + 1], col, carry, left)
                    moves = left | (step + middle + 1 == col)
                    for field in range(5):
                        if field >= 2:
                            state[field, at[part]] = new[field]
                        elif part:
                            state[field, at[part]] = jnp.where(moves, new[field], old[field])

    growing((0, 2), 2)
    growing((2, EDGE_SPLIT), 4)

    start = EAST_END - (HALO + COLS - 1)

    @pl.loop(EDGE_SPLIT, STEPS)
    def _(step):
        begin = HALO + COLS - 1 - step
        x, c, _ = stored_strains(step, step + (start + 1), begin - 1)
        carry = forces(step + start, begin) + (x, c)
        west_carry = forces(step, step) + (blank, blank)
        for part in range(8):
            new, carry = advance(step, step + (start - part), step + (start - part - 1), begin + part, carry)
            west_new, west_carry = advance(step, step + part, step + part + 1, step + part, west_carry)
            for field in range(5):
                state[field, step + (start - part)] = new[field]
                state[field, step + part] = west_new[field]
        u, v = velocities(*west_carry[2:], *stored_strains(step, step + 8, step + 8))
        state[0, step + 8] = u
        state[1, step + 8] = v

    @pl.loop(0, 8)
    def _(at):
        for field in range(5):
            for half in range(2):
                tile = SHRINK * state[field, (HALO + at, EAST_END - HALO - 8 - at)[half]]
                even, odd = column_slices(at, half)
                out[field, even, :] = tile[:8]
                out[field, odd, :] = tile[8:]


def join(parts, passed):
    whole = pl.BlockSpec(memory_space=pltpu.VMEM)
    size = sum(part.shape[0] for part in parts)
    held, *passed = pl.pallas_call(
        functools.partial(join_kernel, len(parts)),
        out_shape=(
            jax.ShapeDtypeStruct((size, *parts[0].shape[1:]), parts[0].dtype),
            *(jax.ShapeDtypeStruct(x.shape, x.dtype) for x in passed),
        ),
        in_specs=[whole] * (len(parts) + len(passed)),
        out_specs=(whole,) * (1 + len(passed)),
        input_output_aliases={len(parts) + k: 1 + k for k in range(len(passed))},
        compiler_params=pltpu.CompilerParams(vmem_limit_bytes=16 * 1024 * 1024),
    )(*parts, *passed)
    return held, passed


def gather_stages(count):
    stages = [(1,)]
    bit = 4
    while bit < count:
        stages.append((3 * bit, 2 * bit, bit) if 2 * bit < count else (bit,))
        bit *= 4
    return stages + [(2,)]


def exchange(held, steps, count):
    return [held] + [lax.ppermute(held, "lon", [(i, i ^ step) for i in range(count)]) for step in steps]


def on_device(final_cot, strains, strength, mass, ice_mask, partner):
    count = lax.axis_size("lon")
    whole = pl.BlockSpec(memory_space=pltpu.VMEM)
    hbm = pl.BlockSpec(memory_space=pltpu.HBM)
    f32 = jnp.float32
    bf16 = jnp.bfloat16
    params = pltpu.CompilerParams(vmem_limit_bytes=16 * 1024 * 1024)
    cells = [
        pltpu.with_memory_space_constraint(x, pltpu.HBM)
        for x in (as_rows(final_cot), strains, strength, mass, ice_mask, partner)
    ]
    state_shape = cells[0].shape
    extended = (
        jax.ShapeDtypeStruct((5, EXT, TILE, LANES), f32),
        jax.ShapeDtypeStruct((STEPS, EXT, TILE, LANES), f32),
        jax.ShapeDtypeStruct((EXT, TILE, LANES), f32),
    )
    sends = (
        jax.ShapeDtypeStruct((WEST_SIZE, TILE, LANES), bf16),
        jax.ShapeDtypeStruct((EAST_SIZE, TILE, LANES), bf16),
    )
    strip, own_strip, state, zeta, weight = pl.pallas_call(
        pack_kernel,
        out_shape=(
            jax.ShapeDtypeStruct((1, STRIP_PARTS, COLS, LANES), bf16),
            jax.ShapeDtypeStruct((1, STRIP_PARTS, COLS, LANES), f32),
            *extended,
        ),
        in_specs=[hbm] * 6,
        out_specs=(whole,) * 5,
        scratch_shapes=[
            pltpu.VMEM(state_shape, f32),
            pltpu.VMEM(strains.shape, bf16),
            pltpu.VMEM(strength.shape, f32),
            pltpu.VMEM(mass.shape, f32),
            pltpu.VMEM(ice_mask.shape, jnp.int32),
            pltpu.SMEM(partner.shape, jnp.int32),
            pltpu.VMEM((2, 256, LANES), f32),
            pltpu.VMEM((6 + STEPS, COLS, LANES), f32),
            pltpu.SemaphoreType.DMA((5 + STEPS // 2,)),
        ],
        compiler_params=params,
    )(*cells)
    stages = gather_stages(count)
    offsets = [0]
    for steps in stages:
        offsets = [offset ^ step for step in (0, *steps) for offset in offsets]
    parts = exchange(strip, stages[0], count)
    state, west_send, east_send = pl.pallas_call(
        first_inner_kernel,
        out_shape=(extended[0], *sends),
        in_specs=[whole] * 3,
        out_specs=(whole,) * 3,
        input_output_aliases={0: 0},
        compiler_params=params,
    )(state, zeta, weight)
    held, (west_send, east_send) = join(parts, (west_send, east_send))
    west = lax.ppermute(west_send, "lon", [(i, (i + 1) % count) for i in range(count)])
    east = lax.ppermute(east_send, "lon", [(i, (i - 1) % count) for i in range(count)])
    state, _ = pl.pallas_call(
        second_inner_kernel,
        out_shape=(extended[0], extended[0]),
        in_specs=[whole] * 3,
        out_specs=(whole,) * 2,
        input_output_aliases={0: 1},
        compiler_params=params,
        cost_estimate=pl.CostEstimate(flops=1000000000, bytes_accessed=1000000000, transcendentals=0),
    )(state, zeta, weight)
    for steps in stages[1:]:
        parts = exchange(held, steps, count)
        if steps != stages[-1]:
            held, (state,) = join(parts, (state,))
    out, *_ = pl.pallas_call(
        edge_kernel,
        out_shape=(jax.ShapeDtypeStruct(state_shape, f32), *extended),
        in_specs=[whole] * 5,
        out_specs=(whole,) * 4,
        input_output_aliases={2: 1, 3: 2, 4: 3},
        compiler_params=params,
    )(west, east, state, zeta, weight)
    out = pl.pallas_call(
        functools.partial(fold_kernel, offsets),
        out_shape=jax.ShapeDtypeStruct(state_shape, f32),
        in_specs=[whole] * (len(parts) + 2),
        out_specs=hbm,
        scratch_shapes=[
            pltpu.VMEM((count, STRIP_PARTS, COLS, LANES), f32),
            pltpu.VMEM((5, COLS, LANES), f32),
            pltpu.SemaphoreType.DMA((4,)),
        ],
        compiler_params=params,
    )(*parts, own_strip, out)
    return from_rows(out)


def solution(mesh):
    return jax.shard_map(
        on_device,
        mesh=mesh,
        in_specs=(
            P("ens", "lon", None),
            P("ens", None, "lon", None),
            P("lon", None),
            P("lon", None),
            P("lon", None),
            P("lon"),
        ),
        out_specs=P("ens", "lon", None),
        check_vma=False,
    )
```

```python
import functools

import jax
import jax.numpy as jnp
from jax import lax
from jax.experimental import pallas as pl
from jax.experimental.pallas import tpu as pltpu
from jax.sharding import PartitionSpec as P

COLS = 16
STEPS = 8
HALO = 8
TILE = 16
LANES = 128
GROUPS = 16
EXT = 40
UNROLL = 8

WEST_COLS = [4, 5, 6, 7]
EAST_COLS = [24, 25, 26, 27]


def numbered(entries):
    return {entry: at for at, entry in enumerate(entries)}


WEST_PLACES = numbered(
    [("state", field, col) for field in range(5) for col in WEST_COLS]
    + [("state", field, 3) for field in range(2, 5)]
    + [("mass", 0, col) for col in WEST_COLS]
    + [
        ("zeta", step, col)
        for step in range(STEPS)
        for col in range(6 - step if step < 4 else step, 8)
    ]
)
EAST_PLACES = numbered(
    [("state", field, col) for field in range(5) for col in EAST_COLS]
    + [("mass", 0, col) for col in EAST_COLS]
    + [
        ("zeta", step, col)
        for step in range(STEPS)
        for col in range(24, 25 + step if step < 4 else 31 - step)
    ]
)
WEST_RESTS = [("state", field, 7) for field in range(2, 5)] + [("zeta", step, 7) for step in range(2)]
EAST_RESTS = [("state", 0, 24), ("state", 1, 24), ("mass", 0, 24)]
WEST_SIZE = len(WEST_PLACES) + len(WEST_RESTS)
EAST_SIZE = len(EAST_PLACES) + len(EAST_RESTS)
STRIP = 16
STRIP_PARTS = 2
STRIP_BEFORE = 6 * STRIP
STRIP_PLACE = STRIP_BEFORE + 8
EAST_END = EXT + 7
EDGE_SPLIT = 4
SHRINK = (5.0 / 6.0) ** STEPS


def as_rows(field):
    lead = field.shape[:-2]
    tiled = field.reshape(lead + (2, 8, GROUPS, LANES)).swapaxes(-3, -2)
    return tiled.reshape(lead + (2 * GROUPS * 8, LANES))


def from_rows(field):
    lead = field.shape[:-2]
    tiled = field.reshape(lead + (2, GROUPS, 8, LANES)).swapaxes(-3, -2)
    return tiled.reshape(lead + (COLS, GROUPS * LANES))


def column_slices(col, half):
    start = half * 128 + col
    return pl.ds(start, 8, 16), pl.ds(start + 8, 8, 16)


def column_tile(load, col, half):
    even, odd = column_slices(col, half)
    return jnp.concatenate([load(even), load(odd)], axis=0)


def viscosity(rates, strength):
    square = rates[0] * rates[0] + 0.25 * (rates[1] * rates[1] + rates[2] * rates[2])
    return (0.1 * strength) * lax.rsqrt(jnp.maximum(square, 0.25))


def pack_kernel(
    state_hbm, strains_hbm, strength_hbm, mass_hbm, mask_hbm, partner_hbm,
    strip_out, own_out, state_out, zeta_out, mass_out,
    state, strains, strength, mass, mask, partner, rows, top, sems,
):
    bf16 = jnp.bfloat16
    cell_copies = [
        pltpu.make_async_copy(mass_hbm, mass, sems.at[0]),
        pltpu.make_async_copy(mask_hbm, mask, sems.at[1]),
    ]
    state_copy = pltpu.make_async_copy(state_hbm, state, sems.at[2])
    late_copies = [
        pltpu.make_async_copy(strength_hbm, strength, sems.at[3]),
        pltpu.make_async_copy(partner_hbm, partner, sems.at[4]),
    ]
    strain_copies = [
        pltpu.make_async_copy(strains_hbm.at[2 * k : 2 * k + 2], strains.at[2 * k : 2 * k + 2], sems.at[5 + k])
        for k in range(STEPS // 2)
    ]
    for copy in [*cell_copies, state_copy, *late_copies, *strain_copies]:
        copy.start()

    for copy in cell_copies:
        copy.wait()
    for group in range(GROUPS):
        at = slice(LANES * group, LANES * group + LANES)
        weight = mask[:, at].astype(jnp.float32) / (6.0 * mass[:, at])
        rows[0, 8 * group : 8 * group + 8] = weight[:8]
        rows[0, 128 + 8 * group : 136 + 8 * group] = weight[8:]
    top[5] = weight
    for at in range(8):
        tile = column_tile(lambda part: rows[0, part, :], at, 0)
        mass_out[HALO + at] = tile
        tile = column_tile(lambda part: rows[0, part, :], at, 1)
        mass_out[HALO + 8 + at] = tile
    state_copy.wait()

    @pl.loop(0, 8)
    def _(at):
        for field in range(5):
            state_out[field, HALO + at] = column_tile(lambda part: state[field, part, :], at, 0)
            state_out[field, HALO + 8 + at] = column_tile(lambda part: state[field, part, :], at, 1)

    for field in range(5):
        top[field, :8] = state[field, 120:128, :]
        top[field, 8:] = state[field, 248:256, :]
    for copy in late_copies:
        copy.wait()

    def cycle_zeta(cycle, step, rows):
        for group in range(GROUPS):
            at = slice(LANES * group, LANES * group + LANES)
            rates = [strains[cycle, k, :, at].astype(jnp.float32) for k in range(3)]
            zeta = viscosity(rates, strength[:, at])
            rows[8 * group : 8 * group + 8] = zeta[:8]
            rows[128 + 8 * group : 136 + 8 * group] = zeta[8:]
        top[6 + step] = zeta
        for at in range(8):
            zeta_out[step, HALO + at] = column_tile(lambda part: rows[part, :], at, 0)
            zeta_out[step, HALO + 8 + at] = column_tile(lambda part: rows[part, :], at, 1)

    @pl.loop(0, STEPS // 2)
    def _(turn):
        pltpu.make_async_copy(
            strains_hbm.at[pl.ds(2 * turn, 2)], strains.at[pl.ds(2 * turn, 2)], sems.at[5 + turn]
        ).wait()
        for part in range(2):
            cycle = 2 * turn + part
            cycle_zeta(cycle, STEPS - 1 - cycle, rows.at[part])

    lane = lax.broadcasted_iota(jnp.int32, (COLS, LANES), 1)
    row_at = lax.broadcasted_iota(jnp.int32, (COLS, LANES), 0)
    place = jnp.zeros((COLS, LANES), jnp.int32)
    for col in range(COLS):
        place = jnp.where(row_at == col, lax.rem(partner[col], COLS), place)
    strips = [jnp.where(lane == STRIP_PLACE, place.astype(jnp.float32), 0.0)] + [jnp.zeros((COLS, LANES), jnp.float32)] * (STRIP_PARTS - 1)
    for at in range(6 + STEPS):
        part, begin = (0, STRIP * at) if at < 6 else (1, STRIP * (at - 6))
        moved = pltpu.roll(top[at], (begin + STRIP) % LANES, 1)
        strips[part] = jnp.where((lane >= begin) & (lane < begin + STRIP), moved, strips[part])
    for k, at in enumerate((0, 1, 5)):
        moved = pltpu.roll(top[at], (STRIP_BEFORE + k + STRIP + 1) % LANES, 1)
        strips[0] = jnp.where(lane == STRIP_BEFORE + k, moved, strips[0])
    for part in range(STRIP_PARTS):
        own_out[0, part] = strips[part]
        strip_out[0, part] = strips[part].astype(bf16)


def join_kernel(count, *refs):
    out = refs[(len(refs) + count - 1) // 2]
    at = 0
    for part in refs[:count]:
        size = part.shape[0]
        out[at : at + size] = part[...]
        at += size


def fold_kernel(offsets, *refs):
    *parts, own, result, out, strips, turned, tiles, sems = refs
    copies = [
        pltpu.make_async_copy(result.at[:, pl.ds(at, 120), :], out.at[:, pl.ds(at, 120), :], sems.at[at // 128])
        for at in (0, 128)
    ]
    for copy in copies:
        copy.start()
    me = lax.axis_index("lon")
    blocks = strips.shape[0]
    total = blocks * COLS
    count = total // LANES
    order = iter(offsets)
    for part in parts:
        for k in range(part.shape[0]):
            strips[next(order)] = part[k].astype(jnp.float32)
    strips[0] = own[0]
    for part in range(STRIP_PARTS):
        for r in range(count):
            group = [strips[lax.bitwise_xor(me, 8 * r + k), part] for k in range(8)]
            turned[part, :, LANES * r : LANES * r + LANES] = jnp.concatenate(group, axis=0).T

    def field(at):
        part, begin = (0, STRIP * at) if at < 6 else (1, STRIP * (at - 6))
        return turned[part, begin : begin + STRIP, :]

    lane = lax.broadcasted_iota(jnp.int32, (8, LANES), 1)
    row = lax.broadcasted_iota(jnp.int32, (STRIP, total), 0)
    last = row == STRIP - 1
    far_row = lax.broadcasted_iota(jnp.int32, (8, total), 0) == 7
    places = [
        (7 - lane // COLS) * COLS
        + jnp.broadcast_to(
            turned[0, STRIP_PLACE : STRIP_PLACE + 1, LANES * r : LANES * r + LANES], (8, LANES)
        ).astype(jnp.int32)
        for r in range(count)
    ]

    def at_fold(value):
        rows = [
            jnp.take_along_axis(
                value[8:, LANES * (count - 1 - r) : LANES * (count - r)], places[r], axis=1,
                mode="promise_in_bounds",
            )
            for r in range(count)
        ]
        far = jnp.where(far_row, jnp.concatenate(rows, axis=1), 0.0)
        return jnp.concatenate([jnp.zeros((8, total), jnp.float32), far], axis=0)

    def next_col(value):
        return pltpu.roll(value, total - 1, 1)

    def prev_col(value):
        return pltpu.roll(value, 1, 1)

    def row_above(value):
        return jnp.where(last, 0.0, pltpu.roll(value, STRIP - 1, 0))

    def row_below(value):
        return pltpu.roll(value, 1, 0)

    vel_u, vel_v, one, two, shear, weight = (field(at) for at in range(6))
    before = turned[0, STRIP_BEFORE : STRIP_BEFORE + 8, :]
    wet = weight != 0.0
    for step in range(STEPS):
        p = weight * vel_u
        q = weight * vel_v
        low_p = row_below(p)
        low_q = row_below(q)
        if step == 0:
            low_p = jnp.where(row == 0, before[2:3] * before[0:1], low_p)
            low_q = jnp.where(row == 0, before[2:3] * before[1:2], low_q)
        along = 0.5 * (p - next_col(p))
        across = 0.5 * (low_q - q + at_fold(q))
        one = one + (along + across)
        two = two + (along - across)
        shear = shear + (low_p - p - at_fold(p)) + (q - next_col(q))
        zeta = field(6 + step)
        first = zeta * one
        quarter = 0.25 * zeta
        second = quarter * two
        third = quarter * shear
        x = first + second
        y = first - second
        wet_u = jnp.where(wet, vel_u, 0.0)
        wet_v = jnp.where(wet, vel_v, 0.0)
        vel_u = (wet_u - 0.1 * wet_v) + (prev_col(x) - x) + (third - row_above(third))
        vel_v = (wet_v + 0.1 * wet_u) + (prev_col(third) - third) + (y - row_above(y))

    shift = lax.rem(total - COLS * me, total)
    rows = [pltpu.roll(value, shift, 1)[:, :LANES] for value in (vel_u, vel_v, one, two, shear)]
    rows.append(jnp.zeros((LANES - 80, LANES), jnp.float32))
    top = SHRINK * jnp.concatenate(rows, axis=0).T[:COLS]
    reached = lax.broadcasted_iota(jnp.int32, (COLS, LANES), 1) >= LANES - STEPS - 1
    for field in range(5):
        moved = pltpu.roll(top, LANES - 16 - 16 * field, 1)
        before = jnp.concatenate([result[field, 120:128, :], result[field, 248:256, :]], axis=0)
        tiles[field] = jnp.where(reached, moved, before)
    last_copies = [
        pltpu.make_async_copy(
            tiles.at[:, 8 * half : 8 * half + 8, :], out.at[:, pl.ds(128 * half + 120, 8), :], sems.at[2 + half]
        )
        for half in range(2)
    ]
    for copy in last_copies:
        copy.start()
    copies.extend(last_copies)
    for copy in copies:
        copy.wait()


def stepper(state, zeta, weight):
    vel_u, vel_v, one, two, shear = (state.at[field] for field in range(5))
    lane = lax.broadcasted_iota(jnp.int32, (8, LANES), 1)
    sub = lax.broadcasted_iota(jnp.int32, (8, LANES), 0)
    first_lane = lane == 0
    last_lane = lane == LANES - 1
    top = sub == 0
    bottom = sub == 7

    def row_above(value):
        turned = pltpu.roll(value, LANES - 1, 1)
        even, odd = turned[:8], turned[8:]
        carried = jnp.where(bottom, 0.0, pltpu.roll(even, 7, 0))
        return jnp.concatenate([jnp.where(last_lane, odd, even), jnp.where(last_lane, carried, odd)], 0)

    def row_below(value):
        turned = pltpu.roll(value, 1, 1)
        even, odd = turned[:8], turned[8:]
        carried = jnp.where(top, 0.0, pltpu.roll(odd, 1, 0))
        return jnp.concatenate([jnp.where(first_lane, carried, even), jnp.where(first_lane, even, odd)], 0)

    def forces(place, col):
        u, v, w = vel_u[place], vel_v[place], weight[col]
        wet = w != 0.0
        wet_u = jnp.where(wet, u, 0.0)
        wet_v = jnp.where(wet, v, 0.0)
        return w * u, w * v, wet_u - 0.1 * wet_v, wet_v + 0.1 * wet_u

    def strains_of(step, col, one_at, two_at, shear_at):
        z = zeta[step, col]
        first = z * one_at
        quarter = 0.25 * z
        second = quarter * two_at
        return first + second, quarter * shear_at, first - second

    def stored_strains(step, place, col):
        return strains_of(step, col, one[place], two[place], shear[place])

    def velocities(keep_u, keep_v, west_x, west_c, x, c, y):
        return keep_u + (west_x - x) + (c - row_above(c)), keep_v + (west_c - c) + (y - row_above(y))

    def advance(step, place, next_place, col, carry, moves=None):
        p, q, keep_u, keep_v, west_x, west_c = carry
        next_p, next_q, next_u, next_v = forces(next_place, col + 1)
        along = 0.5 * (p - next_p)
        across = 0.5 * (row_below(q) - q)
        turn = row_below(p) - p
        new_one = one[place] + (along + across)
        new_two = two[place] + (along - across)
        new_shear = shear[place] + turn + (q - next_q)
        if moves is not None:
            new_one = jnp.where(moves, new_one, one[place])
            new_two = jnp.where(moves, new_two, two[place])
            new_shear = jnp.where(moves, new_shear, shear[place])
        x, c, y = strains_of(step, col, new_one, new_two, new_shear)
        new_u, new_v = velocities(keep_u, keep_v, west_x, west_c, x, c, y)
        return (new_u, new_v, new_one, new_two, new_shear), (next_p, next_q, next_u, next_v, x, c)

    return forces, stored_strains, velocities, advance


def inner_steps(state, zeta, weight, steps, width):
    forces, _, _, advance = stepper(state, zeta, weight)
    blank = jnp.zeros((TILE, LANES), jnp.float32)

    @pl.loop(*steps)
    def _(step):
        begin = HALO + step
        last = HALO + COLS - 2 - step
        carry = forces(begin, begin) + (blank, blank)
        for part in range(width):
            col = begin + part
            new, carry = advance(step, col, col + 1, col, carry)
            for field in range(5):
                valid = (col <= last) & (part > 0) if field < 2 else col <= last
                state[field, col] = jnp.where(valid, new[field], state[field, col])


def first_inner_kernel(state_in, zeta, weight, state, west, east):
    inner_steps(state, zeta, weight, (0, EDGE_SPLIT), COLS - 1)
    for out, places, rests, shift in (
        (west, WEST_PLACES, WEST_RESTS, COLS),
        (east, EAST_PLACES, EAST_RESTS, -COLS),
    ):
        for entry, place in places.items():
            kind, which, col = entry
            source = {"state": state, "zeta": zeta}[kind].at[which] if kind != "mass" else weight
            tile = source[col + shift]
            sent = tile.astype(jnp.bfloat16)
            out[place] = sent
            if entry in rests:
                out[len(places) + rests.index(entry)] = (tile - sent.astype(jnp.float32)).astype(jnp.bfloat16)


def second_inner_kernel(state_in, zeta, weight, sides, state):
    inner_steps(state, zeta, weight, (EDGE_SPLIT, STEPS), COLS - 1 - 2 * EDGE_SPLIT)

    @pl.loop(0, 9)
    def _(at):
        for field in range(5):
            sides[field, HALO + at] = state[field, HALO + at]
            sides[field, EAST_END - HALO - 7 - at] = state[field, HALO + 7 + at]


def edge_kernel(west, east, state_in, zeta_in, mass_in, out, state, zeta, weight):
    for source, places, rests in ((west, WEST_PLACES, WEST_RESTS), (east, EAST_PLACES, EAST_RESTS)):
        for entry, place in places.items():
            kind, which, col = entry
            tile = source[place].astype(jnp.float32)
            if entry in rests:
                tile = tile + source[len(places) + rests.index(entry)].astype(jnp.float32)
            if kind == "state":
                state[which, EAST_END - col if col >= HALO + COLS else col] = tile
            elif kind == "mass":
                weight[col] = tile
            else:
                zeta[which, col] = tile

    forces, stored_strains, velocities, advance = stepper(state, zeta, weight)
    blank = jnp.zeros((TILE, LANES), jnp.float32)

    def growing(steps, reach):
        @pl.loop(*steps)
        def _(step):
            for middle in (HALO - 1, HALO + COLS - 1):
                cols = range(middle - reach, middle + reach + 2)
                at = [col if middle < HALO else EAST_END - col for col in range(cols[0], cols[-1] + 2)]
                carry = forces(at[0], cols[0]) + (blank, blank)
                for part, col in enumerate(cols):
                    old = [state[field, at[part]] for field in range(5)]
                    left = abs(col - middle) <= step
                    new, carry = advance(step, at[part], at[part + 1], col, carry, left)
                    moves = left | (step + middle + 1 == col)
                    for field in range(5):
                        if field >= 2:
                            state[field, at[part]] = new[field]
                        elif part:
                            state[field, at[part]] = jnp.where(moves, new[field], old[field])

    growing((0, 2), 2)
    growing((2, EDGE_SPLIT), 4)

    start = EAST_END - (HALO + COLS - 1)

    @pl.loop(EDGE_SPLIT, STEPS)
    def _(step):
        begin = HALO + COLS - 1 - step
        x, c, _ = stored_strains(step, step + (start + 1), begin - 1)
        carry = forces(step + start, begin) + (x, c)
        west_carry = forces(step, step) + (blank, blank)
        for part in range(8):
            new, carry = advance(step, step + (start - part), step + (start - part - 1), begin + part, carry)
            west_new, west_carry = advance(step, step + part, step + part + 1, step + part, west_carry)
            for field in range(5):
                state[field, step + (start - part)] = new[field]
                state[field, step + part] = west_new[field]
        u, v = velocities(*west_carry[2:], *stored_strains(step, step + 8, step + 8))
        state[0, step + 8] = u
        state[1, step + 8] = v

    @pl.loop(0, 8)
    def _(at):
        for field in range(5):
            for half in range(2):
                tile = SHRINK * state[field, (HALO + at, EAST_END - HALO - 8 - at)[half]]
                even, odd = column_slices(at, half)
                out[field, even, :] = tile[:8]
                out[field, odd, :] = tile[8:]


def join(parts, passed):
    whole = pl.BlockSpec(memory_space=pltpu.VMEM)
    size = sum(part.shape[0] for part in parts)
    held, *passed = pl.pallas_call(
        functools.partial(join_kernel, len(parts)),
        out_shape=(
            jax.ShapeDtypeStruct((size, *parts[0].shape[1:]), parts[0].dtype),
            *(jax.ShapeDtypeStruct(x.shape, x.dtype) for x in passed),
        ),
        in_specs=[whole] * (len(parts) + len(passed)),
        out_specs=(whole,) * (1 + len(passed)),
        input_output_aliases={len(parts) + k: 1 + k for k in range(len(passed))},
        compiler_params=pltpu.CompilerParams(vmem_limit_bytes=16 * 1024 * 1024),
    )(*parts, *passed)
    return held, passed


def gather_stages(count):
    stages = [(1,)]
    bit = 4
    while bit < count:
        stages.append((2 * bit, 3 * bit, bit) if 2 * bit < count else (bit,))
        bit *= 4
    return stages + [(2,)]


def exchange(held, steps, count):
    return [held] + [lax.ppermute(held, "lon", [(i, i ^ step) for i in range(count)]) for step in steps]


def on_device(final_cot, strains, strength, mass, ice_mask, partner):
    count = lax.axis_size("lon")
    whole = pl.BlockSpec(memory_space=pltpu.VMEM)
    hbm = pl.BlockSpec(memory_space=pltpu.HBM)
    f32 = jnp.float32
    bf16 = jnp.bfloat16
    params = pltpu.CompilerParams(vmem_limit_bytes=16 * 1024 * 1024)
    cells = [
        pltpu.with_memory_space_constraint(x, pltpu.HBM)
        for x in (as_rows(final_cot), strains, strength, mass, ice_mask, partner)
    ]
    state_shape = cells[0].shape
    extended = (
        jax.ShapeDtypeStruct((5, EXT, TILE, LANES), f32),
        jax.ShapeDtypeStruct((STEPS, EXT, TILE, LANES), f32),
        jax.ShapeDtypeStruct((EXT, TILE, LANES), f32),
    )
    sends = (
        jax.ShapeDtypeStruct((WEST_SIZE, TILE, LANES), bf16),
        jax.ShapeDtypeStruct((EAST_SIZE, TILE, LANES), bf16),
    )
    strip, own_strip, state, zeta, weight = pl.pallas_call(
        pack_kernel,
        out_shape=(
            jax.ShapeDtypeStruct((1, STRIP_PARTS, COLS, LANES), bf16),
            jax.ShapeDtypeStruct((1, STRIP_PARTS, COLS, LANES), f32),
            *extended,
        ),
        in_specs=[hbm] * 6,
        out_specs=(whole,) * 5,
        scratch_shapes=[
            pltpu.VMEM(state_shape, f32),
            pltpu.VMEM(strains.shape, bf16),
            pltpu.VMEM(strength.shape, f32),
            pltpu.VMEM(mass.shape, f32),
            pltpu.VMEM(ice_mask.shape, jnp.int32),
            pltpu.SMEM(partner.shape, jnp.int32),
            pltpu.VMEM((2, 256, LANES), f32),
            pltpu.VMEM((6 + STEPS, COLS, LANES), f32),
            pltpu.SemaphoreType.DMA((5 + STEPS // 2,)),
        ],
        compiler_params=params,
    )(*cells)
    stages = gather_stages(count)
    offsets = [0]
    for steps in stages:
        offsets = [offset ^ step for step in (0, *steps) for offset in offsets]
    parts = exchange(strip, stages[0], count)
    state, west_send, east_send = pl.pallas_call(
        first_inner_kernel,
        out_shape=(extended[0], *sends),
        in_specs=[whole] * 3,
        out_specs=(whole,) * 3,
        input_output_aliases={0: 0},
        compiler_params=params,
    )(state, zeta, weight)
    held, (west_send, east_send) = join(parts, (west_send, east_send))
    west = lax.ppermute(west_send, "lon", [(i, (i + 1) % count) for i in range(count)])
    east = lax.ppermute(east_send, "lon", [(i, (i - 1) % count) for i in range(count)])
    state, _ = pl.pallas_call(
        second_inner_kernel,
        out_shape=(extended[0], extended[0]),
        in_specs=[whole] * 3,
        out_specs=(whole,) * 2,
        input_output_aliases={0: 1},
        compiler_params=params,
        cost_estimate=pl.CostEstimate(flops=1500000000, bytes_accessed=0, transcendentals=0),
    )(state, zeta, weight)
    for steps in stages[1:]:
        parts = exchange(held, steps, count)
        if steps != stages[-1]:
            held, (state,) = join(parts, (state,))
    out, *_ = pl.pallas_call(
        edge_kernel,
        out_shape=(jax.ShapeDtypeStruct(state_shape, f32), *extended),
        in_specs=[whole] * 5,
        out_specs=(whole,) * 4,
        input_output_aliases={2: 1, 3: 2, 4: 3},
        compiler_params=params,
    )(west, east, state, zeta, weight)
    out = pl.pallas_call(
        functools.partial(fold_kernel, offsets),
        out_shape=jax.ShapeDtypeStruct(state_shape, f32),
        in_specs=[whole] * (len(parts) + 2),
        out_specs=hbm,
        scratch_shapes=[
            pltpu.VMEM((count, STRIP_PARTS, COLS, LANES), f32),
            pltpu.VMEM((STRIP_PARTS, LANES, count * COLS), f32),
            pltpu.VMEM((5, COLS, LANES), f32),
            pltpu.SemaphoreType.DMA((4,)),
        ],
        compiler_params=params,
    )(*parts, own_strip, out)
    return from_rows(out)


def solution(mesh):
    return jax.shard_map(
        on_device,
        mesh=mesh,
        in_specs=(
            P("ens", "lon", None),
            P("ens", None, "lon", None),
            P("lon", None),
            P("lon", None),
            P("lon", None),
            P("lon"),
        ),
        out_specs=P("ens", "lon", None),
        check_vma=False,
    )
```

```python
import functools

import jax
import jax.numpy as jnp
from jax import lax
from jax.experimental import pallas as pl
from jax.experimental.pallas import tpu as pltpu
from jax.sharding import PartitionSpec as P

COLS = 16
STEPS = 8
HALO = 8
TILE = 16
LANES = 128
GROUPS = 16
EXT = 40
UNROLL = 8

WEST_COLS = [4, 5, 6, 7]
EAST_COLS = [24, 25, 26, 27]


def numbered(entries):
    return {entry: at for at, entry in enumerate(entries)}


WEST_PLACES = numbered(
    [("state", field, col) for field in range(5) for col in WEST_COLS]
    + [("state", field, 3) for field in range(2, 5)]
    + [("mass", 0, col) for col in WEST_COLS]
    + [
        ("zeta", step, col)
        for step in range(STEPS)
        for col in range(6 - step if step < 4 else step, 8)
    ]
)
EAST_PLACES = numbered(
    [("state", field, col) for field in range(5) for col in EAST_COLS]
    + [("mass", 0, col) for col in EAST_COLS]
    + [
        ("zeta", step, col)
        for step in range(STEPS)
        for col in range(24, 25 + step if step < 4 else 31 - step)
    ]
)
WEST_RESTS = [("state", field, 7) for field in range(2, 5)] + [("zeta", step, 7) for step in range(2)]
EAST_RESTS = [("state", 0, 24), ("state", 1, 24), ("mass", 0, 24)]
WEST_SIZE = len(WEST_PLACES) + len(WEST_RESTS)
EAST_SIZE = len(EAST_PLACES) + len(EAST_RESTS)
STRIP = 16
STRIP_PARTS = 2
STRIP_BEFORE = 6 * STRIP
STRIP_PLACE = STRIP_BEFORE + 8
EAST_END = EXT + 7
EDGE_SPLIT = 4
SHRINK = (5.0 / 6.0) ** STEPS


def as_rows(field):
    lead = field.shape[:-2]
    tiled = field.reshape(lead + (2, 8, GROUPS, LANES)).swapaxes(-3, -2)
    return tiled.reshape(lead + (2 * GROUPS * 8, LANES))


def from_rows(field):
    lead = field.shape[:-2]
    tiled = field.reshape(lead + (2, GROUPS, 8, LANES)).swapaxes(-3, -2)
    return tiled.reshape(lead + (COLS, GROUPS * LANES))


def column_slices(col, half):
    start = half * 128 + col
    return pl.ds(start, 8, 16), pl.ds(start + 8, 8, 16)


def column_tile(load, col, half):
    even, odd = column_slices(col, half)
    return jnp.concatenate([load(even), load(odd)], axis=0)


def viscosity(rates, strength):
    square = rates[0] * rates[0] + 0.25 * (rates[1] * rates[1] + rates[2] * rates[2])
    return (0.1 * strength) * lax.rsqrt(jnp.maximum(square, 0.25))


def pack_kernel(
    state_hbm, strains_hbm, strength_hbm, mass_hbm, mask_hbm, partner_hbm,
    strip_out, own_out, state_out, zeta_out, mass_out,
    state, strains, strength, mass, mask, partner, rows, top, sems,
):
    bf16 = jnp.bfloat16
    cell_copies = [
        pltpu.make_async_copy(mass_hbm, mass, sems.at[0]),
        pltpu.make_async_copy(mask_hbm, mask, sems.at[1]),
    ]
    state_copy = pltpu.make_async_copy(state_hbm, state, sems.at[2])
    late_copies = [
        pltpu.make_async_copy(strength_hbm, strength, sems.at[3]),
        pltpu.make_async_copy(partner_hbm, partner, sems.at[4]),
    ]
    strain_copies = [
        pltpu.make_async_copy(strains_hbm.at[2 * k : 2 * k + 2], strains.at[2 * k : 2 * k + 2], sems.at[5 + k])
        for k in range(STEPS // 2)
    ]
    for copy in [*cell_copies, state_copy, *late_copies, *strain_copies]:
        copy.start()

    for copy in cell_copies:
        copy.wait()
    for group in range(GROUPS):
        at = slice(LANES * group, LANES * group + LANES)
        weight = mask[:, at].astype(jnp.float32) / (6.0 * mass[:, at])
        rows[0, 8 * group : 8 * group + 8] = weight[:8]
        rows[0, 128 + 8 * group : 136 + 8 * group] = weight[8:]
    top[5] = weight
    for at in range(8):
        tile = column_tile(lambda part: rows[0, part, :], at, 0)
        mass_out[HALO + at] = tile
        tile = column_tile(lambda part: rows[0, part, :], at, 1)
        mass_out[HALO + 8 + at] = tile
    state_copy.wait()

    @pl.loop(0, 8)
    def _(at):
        for field in range(5):
            state_out[field, HALO + at] = column_tile(lambda part: state[field, part, :], at, 0)
            state_out[field, HALO + 8 + at] = column_tile(lambda part: state[field, part, :], at, 1)

    for field in range(5):
        top[field, :8] = state[field, 120:128, :]
        top[field, 8:] = state[field, 248:256, :]
    for copy in late_copies:
        copy.wait()

    def cycle_zeta(cycle, step, rows):
        for group in range(GROUPS):
            at = slice(LANES * group, LANES * group + LANES)
            rates = [strains[cycle, k, :, at].astype(jnp.float32) for k in range(3)]
            zeta = viscosity(rates, strength[:, at])
            rows[8 * group : 8 * group + 8] = zeta[:8]
            rows[128 + 8 * group : 136 + 8 * group] = zeta[8:]
        top[6 + step] = zeta
        for at in range(8):
            zeta_out[step, HALO + at] = column_tile(lambda part: rows[part, :], at, 0)
            zeta_out[step, HALO + 8 + at] = column_tile(lambda part: rows[part, :], at, 1)

    @pl.loop(0, STEPS // 2)
    def _(turn):
        pltpu.make_async_copy(
            strains_hbm.at[pl.ds(2 * turn, 2)], strains.at[pl.ds(2 * turn, 2)], sems.at[5 + turn]
        ).wait()
        for part in range(2):
            cycle = 2 * turn + part
            cycle_zeta(cycle, STEPS - 1 - cycle, rows.at[part])

    lane = lax.broadcasted_iota(jnp.int32, (COLS, LANES), 1)
    row_at = lax.broadcasted_iota(jnp.int32, (COLS, LANES), 0)
    place = jnp.zeros((COLS, LANES), jnp.int32)
    for col in range(COLS):
        place = jnp.where(row_at == col, lax.rem(partner[col], COLS), place)
    strips = [jnp.where(lane == STRIP_PLACE, place.astype(jnp.float32), 0.0)] + [jnp.zeros((COLS, LANES), jnp.float32)] * (STRIP_PARTS - 1)
    for at in range(6 + STEPS):
        part, begin = (0, STRIP * at) if at < 6 else (1, STRIP * (at - 6))
        moved = pltpu.roll(top[at], (begin + STRIP) % LANES, 1)
        strips[part] = jnp.where((lane >= begin) & (lane < begin + STRIP), moved, strips[part])
    for k, at in enumerate((0, 1, 5)):
        moved = pltpu.roll(top[at], (STRIP_BEFORE + k + STRIP + 1) % LANES, 1)
        strips[0] = jnp.where(lane == STRIP_BEFORE + k, moved, strips[0])
    for part in range(STRIP_PARTS):
        own_out[0, part] = strips[part]
        strip_out[0, part] = strips[part].astype(bf16)


def join_kernel(count, *refs):
    out = refs[(len(refs) + count - 1) // 2]
    at = 0
    for part in refs[:count]:
        size = part.shape[0]
        out[at : at + size] = part[...]
        at += size


def fold_kernel(offsets, *refs):
    *parts, own, result, out, strips, turned, tiles, sems = refs
    copies = [
        pltpu.make_async_copy(result.at[:, pl.ds(at, 120), :], out.at[:, pl.ds(at, 120), :], sems.at[at // 128])
        for at in (0, 128)
    ]
    for copy in copies:
        copy.start()
    me = lax.axis_index("lon")
    blocks = strips.shape[0]
    total = blocks * COLS
    count = total // LANES
    order = iter(offsets)
    for part in parts:
        for k in range(part.shape[0]):
            strips[next(order)] = part[k].astype(jnp.float32)
    strips[0] = own[0]
    for part in range(STRIP_PARTS):
        for r in range(count):
            group = [strips[lax.bitwise_xor(me, 8 * r + k), part] for k in range(8)]
            turned[part, :, LANES * r : LANES * r + LANES] = jnp.concatenate(group, axis=0).T

    def field(at):
        part, begin = (0, STRIP * at) if at < 6 else (1, STRIP * (at - 6))
        return turned[part, begin : begin + STRIP, :]

    lane = lax.broadcasted_iota(jnp.int32, (8, LANES), 1)
    row = lax.broadcasted_iota(jnp.int32, (STRIP, total), 0)
    last = row == STRIP - 1
    far_row = lax.broadcasted_iota(jnp.int32, (8, total), 0) == 7
    places = [
        (7 - lane // COLS) * COLS
        + jnp.broadcast_to(
            turned[0, STRIP_PLACE : STRIP_PLACE + 1, LANES * r : LANES * r + LANES], (8, LANES)
        ).astype(jnp.int32)
        for r in range(count)
    ]

    def at_fold(value):
        rows = [
            jnp.take_along_axis(
                value[8:, LANES * (count - 1 - r) : LANES * (count - r)], places[r], axis=1,
                mode="promise_in_bounds",
            )
            for r in range(count)
        ]
        far = jnp.where(far_row, jnp.concatenate(rows, axis=1), 0.0)
        return jnp.concatenate([jnp.zeros((8, total), jnp.float32), far], axis=0)

    def next_col(value):
        return pltpu.roll(value, total - 1, 1)

    def prev_col(value):
        return pltpu.roll(value, 1, 1)

    def row_above(value):
        return jnp.where(last, 0.0, pltpu.roll(value, STRIP - 1, 0))

    def row_below(value):
        return pltpu.roll(value, 1, 0)

    vel_u, vel_v, one, two, shear, weight = (field(at) for at in range(6))
    before = turned[0, STRIP_BEFORE : STRIP_BEFORE + 8, :]
    wet = weight != 0.0
    for step in range(STEPS):
        p = weight * vel_u
        q = weight * vel_v
        low_p = row_below(p)
        low_q = row_below(q)
        if step == 0:
            low_p = jnp.where(row == 0, before[2:3] * before[0:1], low_p)
            low_q = jnp.where(row == 0, before[2:3] * before[1:2], low_q)
        along = 0.5 * (p - next_col(p))
        across = 0.5 * (low_q - q + at_fold(q))
        one = one + (along + across)
        two = two + (along - across)
        shear = shear + (low_p - p - at_fold(p)) + (q - next_col(q))
        zeta = field(6 + step)
        first = zeta * one
        quarter = 0.25 * zeta
        second = quarter * two
        third = quarter * shear
        x = first + second
        y = first - second
        wet_u = jnp.where(wet, vel_u, 0.0)
        wet_v = jnp.where(wet, vel_v, 0.0)
        vel_u = (wet_u - 0.1 * wet_v) + (prev_col(x) - x) + (third - row_above(third))
        vel_v = (wet_v + 0.1 * wet_u) + (prev_col(third) - third) + (y - row_above(y))

    shift = lax.rem(total - COLS * me, total)
    rows = [pltpu.roll(value, shift, 1)[:, :LANES] for value in (vel_u, vel_v, one, two, shear)]
    rows.append(jnp.zeros((LANES - 80, LANES), jnp.float32))
    top = SHRINK * jnp.concatenate(rows, axis=0).T[:COLS]
    reached = lax.broadcasted_iota(jnp.int32, (COLS, LANES), 1) >= LANES - STEPS - 1
    for field in range(5):
        moved = pltpu.roll(top, LANES - 16 - 16 * field, 1)
        before = jnp.concatenate([result[field, 120:128, :], result[field, 248:256, :]], axis=0)
        tiles[field] = jnp.where(reached, moved, before)
    last_copies = [
        pltpu.make_async_copy(
            tiles.at[:, 8 * half : 8 * half + 8, :], out.at[:, pl.ds(128 * half + 120, 8), :], sems.at[2 + half]
        )
        for half in range(2)
    ]
    for copy in last_copies:
        copy.start()
    copies.extend(last_copies)
    for copy in copies:
        copy.wait()


def stepper(state, zeta, weight):
    vel_u, vel_v, one, two, shear = (state.at[field] for field in range(5))
    lane = lax.broadcasted_iota(jnp.int32, (8, LANES), 1)
    sub = lax.broadcasted_iota(jnp.int32, (8, LANES), 0)
    first_lane = lane == 0
    last_lane = lane == LANES - 1
    top = sub == 0
    bottom = sub == 7

    def row_above(value):
        turned = pltpu.roll(value, LANES - 1, 1)
        even, odd = turned[:8], turned[8:]
        carried = jnp.where(bottom, 0.0, pltpu.roll(even, 7, 0))
        return jnp.concatenate([jnp.where(last_lane, odd, even), jnp.where(last_lane, carried, odd)], 0)

    def row_below(value):
        turned = pltpu.roll(value, 1, 1)
        even, odd = turned[:8], turned[8:]
        carried = jnp.where(top, 0.0, pltpu.roll(odd, 1, 0))
        return jnp.concatenate([jnp.where(first_lane, carried, even), jnp.where(first_lane, even, odd)], 0)

    def forces(place, col):
        u, v, w = vel_u[place], vel_v[place], weight[col]
        wet = w != 0.0
        wet_u = jnp.where(wet, u, 0.0)
        wet_v = jnp.where(wet, v, 0.0)
        return w * u, w * v, wet_u - 0.1 * wet_v, wet_v + 0.1 * wet_u

    def strains_of(step, col, one_at, two_at, shear_at):
        z = zeta[step, col]
        first = z * one_at
        quarter = 0.25 * z
        second = quarter * two_at
        return first + second, quarter * shear_at, first - second

    def stored_strains(step, place, col):
        return strains_of(step, col, one[place], two[place], shear[place])

    def velocities(keep_u, keep_v, west_x, west_c, x, c, y):
        return keep_u + (west_x - x) + (c - row_above(c)), keep_v + (west_c - c) + (y - row_above(y))

    def advance(step, place, next_place, col, carry):
        p, q, keep_u, keep_v, west_x, west_c = carry
        next_p, next_q, next_u, next_v = forces(next_place, col + 1)
        along = 0.5 * (p - next_p)
        across = 0.5 * (row_below(q) - q)
        turn = row_below(p) - p
        new_one = one[place] + (along + across)
        new_two = two[place] + (along - across)
        new_shear = shear[place] + turn + (q - next_q)
        x, c, y = strains_of(step, col, new_one, new_two, new_shear)
        new_u, new_v = velocities(keep_u, keep_v, west_x, west_c, x, c, y)
        return (new_u, new_v, new_one, new_two, new_shear), (next_p, next_q, next_u, next_v, x, c)

    return forces, stored_strains, velocities, advance


def inner_steps(state, zeta, weight, steps):
    forces, _, _, advance = stepper(state, zeta, weight)
    blank = jnp.zeros((TILE, LANES), jnp.float32)
    for step in steps:
        begin = HALO + step
        carry = forces(begin, begin) + (blank, blank)
        for col in range(begin, HALO + COLS - 1 - step):
            new, carry = advance(step, col, col + 1, col, carry)
            for field in range(2 if col == begin else 0, 5):
                state[field, col] = new[field]


def first_inner_kernel(state_in, zeta, weight, state, west, east):
    inner_steps(state, zeta, weight, range(EDGE_SPLIT))
    for out, places, rests, shift in (
        (west, WEST_PLACES, WEST_RESTS, COLS),
        (east, EAST_PLACES, EAST_RESTS, -COLS),
    ):
        for entry, place in places.items():
            kind, which, col = entry
            source = {"state": state, "zeta": zeta}[kind].at[which] if kind != "mass" else weight
            tile = source[col + shift]
            sent = tile.astype(jnp.bfloat16)
            out[place] = sent
            if entry in rests:
                out[len(places) + rests.index(entry)] = (tile - sent.astype(jnp.float32)).astype(jnp.bfloat16)


def second_inner_kernel(state_in, zeta, weight, sides, state):
    inner_steps(state, zeta, weight, range(EDGE_SPLIT, STEPS))

    @pl.loop(0, 9)
    def _(at):
        for field in range(5):
            sides[field, HALO + at] = state[field, HALO + at]
            sides[field, EAST_END - HALO - 7 - at] = state[field, HALO + 7 + at]


def edge_kernel(west, east, state_in, zeta_in, mass_in, out, state, zeta, weight):
    for source, places, rests in ((west, WEST_PLACES, WEST_RESTS), (east, EAST_PLACES, EAST_RESTS)):
        for entry, place in places.items():
            kind, which, col = entry
            tile = source[place].astype(jnp.float32)
            if entry in rests:
                tile = tile + source[len(places) + rests.index(entry)].astype(jnp.float32)
            if kind == "state":
                state[which, EAST_END - col if col >= HALO + COLS else col] = tile
            elif kind == "mass":
                weight[col] = tile
            else:
                zeta[which, col] = tile

    forces, stored_strains, velocities, advance = stepper(state, zeta, weight)
    blank = jnp.zeros((TILE, LANES), jnp.float32)

    def grow(step):
        for middle in (HALO - 1, HALO + COLS - 1):
            cols = range(middle - step, middle + step + 1)
            at = [col if middle < HALO else EAST_END - col for col in (*cols, middle + step + 1)]
            behind = middle - step - 1
            x, c, _ = stored_strains(step, behind if middle < HALO else EAST_END - behind, behind)
            carry = forces(at[0], cols[0]) + (x, c)
            for part, col in enumerate(cols):
                new, carry = advance(step, at[part], at[part + 1], col, carry)
                for field in range(5):
                    state[field, at[part]] = new[field]
            ahead = middle + step + 1
            state[0, at[-1]], state[1, at[-1]] = velocities(*carry[2:], *stored_strains(step, at[-1], ahead))

    for step in range(EDGE_SPLIT):
        grow(step)

    start = EAST_END - (HALO + COLS - 1)

    @pl.loop(EDGE_SPLIT, STEPS)
    def _(step):
        begin = HALO + COLS - 1 - step
        x, c, _ = stored_strains(step, step + (start + 1), begin - 1)
        carry = forces(step + start, begin) + (x, c)
        west_carry = forces(step, step) + (blank, blank)
        for part in range(8):
            new, carry = advance(step, step + (start - part), step + (start - part - 1), begin + part, carry)
            west_new, west_carry = advance(step, step + part, step + part + 1, step + part, west_carry)
            for field in range(5):
                state[field, step + (start - part)] = new[field]
                state[field, step + part] = west_new[field]
        u, v = velocities(*west_carry[2:], *stored_strains(step, step + 8, step + 8))
        state[0, step + 8] = u
        state[1, step + 8] = v

    @pl.loop(0, 8)
    def _(at):
        for field in range(5):
            for half in range(2):
                tile = SHRINK * state[field, (HALO + at, EAST_END - HALO - 8 - at)[half]]
                even, odd = column_slices(at, half)
                out[field, even, :] = tile[:8]
                out[field, odd, :] = tile[8:]


def join(parts, passed):
    whole = pl.BlockSpec(memory_space=pltpu.VMEM)
    size = sum(part.shape[0] for part in parts)
    held, *passed = pl.pallas_call(
        functools.partial(join_kernel, len(parts)),
        out_shape=(
            jax.ShapeDtypeStruct((size, *parts[0].shape[1:]), parts[0].dtype),
            *(jax.ShapeDtypeStruct(x.shape, x.dtype) for x in passed),
        ),
        in_specs=[whole] * (len(parts) + len(passed)),
        out_specs=(whole,) * (1 + len(passed)),
        input_output_aliases={len(parts) + k: 1 + k for k in range(len(passed))},
        compiler_params=pltpu.CompilerParams(vmem_limit_bytes=16 * 1024 * 1024),
    )(*parts, *passed)
    return held, passed


def gather_stages(count):
    stages = [(1,)]
    bit = 4
    while bit < count:
        stages.append((2 * bit, 3 * bit, bit) if 2 * bit < count else (bit,))
        bit *= 4
    return stages + [(2,)]


def exchange(held, steps, count):
    return [held] + [lax.ppermute(held, "lon", [(i, i ^ step) for i in range(count)]) for step in steps]


def on_device(final_cot, strains, strength, mass, ice_mask, partner):
    count = lax.axis_size("lon")
    whole = pl.BlockSpec(memory_space=pltpu.VMEM)
    hbm = pl.BlockSpec(memory_space=pltpu.HBM)
    f32 = jnp.float32
    bf16 = jnp.bfloat16
    params = pltpu.CompilerParams(vmem_limit_bytes=16 * 1024 * 1024)
    cells = [
        pltpu.with_memory_space_constraint(x, pltpu.HBM)
        for x in (as_rows(final_cot), strains, strength, mass, ice_mask, partner)
    ]
    state_shape = cells[0].shape
    extended = (
        jax.ShapeDtypeStruct((5, EXT, TILE, LANES), f32),
        jax.ShapeDtypeStruct((STEPS, EXT, TILE, LANES), f32),
        jax.ShapeDtypeStruct((EXT, TILE, LANES), f32),
    )
    sends = (
        jax.ShapeDtypeStruct((WEST_SIZE, TILE, LANES), bf16),
        jax.ShapeDtypeStruct((EAST_SIZE, TILE, LANES), bf16),
    )
    strip, own_strip, state, zeta, weight = pl.pallas_call(
        pack_kernel,
        out_shape=(
            jax.ShapeDtypeStruct((1, STRIP_PARTS, COLS, LANES), bf16),
            jax.ShapeDtypeStruct((1, STRIP_PARTS, COLS, LANES), f32),
            *extended,
        ),
        in_specs=[hbm] * 6,
        out_specs=(whole,) * 5,
        scratch_shapes=[
            pltpu.VMEM(state_shape, f32),
            pltpu.VMEM(strains.shape, bf16),
            pltpu.VMEM(strength.shape, f32),
            pltpu.VMEM(mass.shape, f32),
            pltpu.VMEM(ice_mask.shape, jnp.int32),
            pltpu.SMEM(partner.shape, jnp.int32),
            pltpu.VMEM((2, 256, LANES), f32),
            pltpu.VMEM((6 + STEPS, COLS, LANES), f32),
            pltpu.SemaphoreType.DMA((5 + STEPS // 2,)),
        ],
        compiler_params=params,
    )(*cells)
    stages = gather_stages(count)
    offsets = [0]
    for steps in stages:
        offsets = [offset ^ step for step in (0, *steps) for offset in offsets]
    parts = exchange(strip, stages[0], count)
    state, west_send, east_send = pl.pallas_call(
        first_inner_kernel,
        out_shape=(extended[0], *sends),
        in_specs=[whole] * 3,
        out_specs=(whole,) * 3,
        input_output_aliases={0: 0},
        compiler_params=params,
    )(state, zeta, weight)
    held, (west_send, east_send) = join(parts, (west_send, east_send))
    west = lax.ppermute(west_send, "lon", [(i, (i + 1) % count) for i in range(count)])
    east = lax.ppermute(east_send, "lon", [(i, (i - 1) % count) for i in range(count)])
    state, _ = pl.pallas_call(
        second_inner_kernel,
        out_shape=(extended[0], extended[0]),
        in_specs=[whole] * 3,
        out_specs=(whole,) * 2,
        input_output_aliases={0: 1},
        compiler_params=params,
        cost_estimate=pl.CostEstimate(flops=1500000000, bytes_accessed=0, transcendentals=0),
    )(state, zeta, weight)
    for steps in stages[1:]:
        parts = exchange(held, steps, count)
        if steps != stages[-1]:
            held, (state,) = join(parts, (state,))
    out, *_ = pl.pallas_call(
        edge_kernel,
        out_shape=(jax.ShapeDtypeStruct(state_shape, f32), *extended),
        in_specs=[whole] * 5,
        out_specs=(whole,) * 4,
        input_output_aliases={2: 1, 3: 2, 4: 3},
        compiler_params=params,
    )(west, east, state, zeta, weight)
    out = pl.pallas_call(
        functools.partial(fold_kernel, offsets),
        out_shape=jax.ShapeDtypeStruct(state_shape, f32),
        in_specs=[whole] * (len(parts) + 2),
        out_specs=hbm,
        scratch_shapes=[
            pltpu.VMEM((count, STRIP_PARTS, COLS, LANES), f32),
            pltpu.VMEM((STRIP_PARTS, LANES, count * COLS), f32),
            pltpu.VMEM((5, COLS, LANES), f32),
            pltpu.SemaphoreType.DMA((4,)),
        ],
        compiler_params=params,
    )(*parts, own_strip, out)
    return from_rows(out)


def solution(mesh):
    return jax.shard_map(
        on_device,
        mesh=mesh,
        in_specs=(
            P("ens", "lon", None),
            P("ens", None, "lon", None),
            P("lon", None),
            P("lon", None),
            P("lon", None),
            P("lon"),
        ),
        out_specs=P("ens", "lon", None),
        check_vma=False,
    )
```

```python
import functools

import jax
import jax.numpy as jnp
from jax import lax
from jax.experimental import pallas as pl
from jax.experimental.pallas import tpu as pltpu
from jax.sharding import PartitionSpec as P

COLS = 16
STEPS = 8
HALO = 8
TILE = 16
LANES = 128
GROUPS = 16
EXT = 40
UNROLL = 8

WEST_COLS = [4, 5, 6, 7]
EAST_COLS = [24, 25, 26, 27]


def numbered(entries):
    return {entry: at for at, entry in enumerate(entries)}


WEST_PLACES = numbered(
    [("state", field, col) for field in range(5) for col in WEST_COLS]
    + [("state", field, 3) for field in range(2, 5)]
    + [("mass", 0, col) for col in WEST_COLS]
    + [
        ("zeta", step, col)
        for step in range(STEPS)
        for col in range(6 - step if step < 4 else step, 8)
    ]
)
EAST_PLACES = numbered(
    [("state", field, col) for field in range(5) for col in EAST_COLS]
    + [("mass", 0, col) for col in EAST_COLS]
    + [
        ("zeta", step, col)
        for step in range(STEPS)
        for col in range(24, 25 + step if step < 4 else 31 - step)
    ]
)
WEST_RESTS = [("state", field, 7) for field in range(2, 5)] + [("zeta", step, 7) for step in range(2)]
EAST_RESTS = [("state", 0, 24), ("state", 1, 24), ("mass", 0, 24)]
WEST_SIZE = len(WEST_PLACES) + len(WEST_RESTS)
EAST_SIZE = len(EAST_PLACES) + len(EAST_RESTS)
STRIP = 16
STRIP_PARTS = 2
STRIP_BEFORE = 6 * STRIP
STRIP_PLACE = STRIP_BEFORE + 8
EAST_END = EXT + 7
EDGE_SPLIT = 4
SHRINK = (5.0 / 6.0) ** STEPS


def as_rows(field):
    lead = field.shape[:-2]
    tiled = field.reshape(lead + (2, 8, GROUPS, LANES)).swapaxes(-3, -2)
    return tiled.reshape(lead + (2 * GROUPS * 8, LANES))


def from_rows(field):
    lead = field.shape[:-2]
    tiled = field.reshape(lead + (2, GROUPS, 8, LANES)).swapaxes(-3, -2)
    return tiled.reshape(lead + (COLS, GROUPS * LANES))


def column_slices(col, half):
    start = half * 128 + col
    return pl.ds(start, 8, 16), pl.ds(start + 8, 8, 16)


def column_tile(load, col, half):
    even, odd = column_slices(col, half)
    return jnp.concatenate([load(even), load(odd)], axis=0)


def viscosity(rates, strength):
    square = rates[0] * rates[0] + 0.25 * (rates[1] * rates[1] + rates[2] * rates[2])
    return (0.1 * strength) * lax.rsqrt(jnp.maximum(square, 0.25))


def pack_kernel(
    state_hbm, strains_hbm, strength_hbm, mass_hbm, mask_hbm, partner_hbm,
    strip_out, own_out, state_out, zeta_out, mass_out,
    state, strains, strength, mass, mask, partner, rows, top, sems,
):
    bf16 = jnp.bfloat16
    cell_copies = [
        pltpu.make_async_copy(mass_hbm, mass, sems.at[0]),
        pltpu.make_async_copy(mask_hbm, mask, sems.at[1]),
    ]
    state_copy = pltpu.make_async_copy(state_hbm, state, sems.at[2])
    late_copies = [
        pltpu.make_async_copy(strength_hbm, strength, sems.at[3]),
        pltpu.make_async_copy(partner_hbm, partner, sems.at[4]),
    ]
    strain_copies = [
        pltpu.make_async_copy(strains_hbm.at[2 * k : 2 * k + 2], strains.at[2 * k : 2 * k + 2], sems.at[5 + k])
        for k in range(STEPS // 2)
    ]
    for copy in [*cell_copies, state_copy, *late_copies, *strain_copies]:
        copy.start()

    for copy in cell_copies:
        copy.wait()
    for group in range(GROUPS):
        at = slice(LANES * group, LANES * group + LANES)
        weight = mask[:, at].astype(jnp.float32) / (6.0 * mass[:, at])
        rows[0, 8 * group : 8 * group + 8] = weight[:8]
        rows[0, 128 + 8 * group : 136 + 8 * group] = weight[8:]
    top[5] = weight
    for at in range(8):
        tile = column_tile(lambda part: rows[0, part, :], at, 0)
        mass_out[HALO + at] = tile
        tile = column_tile(lambda part: rows[0, part, :], at, 1)
        mass_out[HALO + 8 + at] = tile
    state_copy.wait()

    @pl.loop(0, 8)
    def _(at):
        for field in range(5):
            state_out[field, HALO + at] = column_tile(lambda part: state[field, part, :], at, 0)
            state_out[field, HALO + 8 + at] = column_tile(lambda part: state[field, part, :], at, 1)

    for field in range(5):
        top[field, :8] = state[field, 120:128, :]
        top[field, 8:] = state[field, 248:256, :]
    for copy in late_copies:
        copy.wait()

    def cycle_zeta(cycle, step, rows):
        for group in range(GROUPS):
            at = slice(LANES * group, LANES * group + LANES)
            rates = [strains[cycle, k, :, at].astype(jnp.float32) for k in range(3)]
            zeta = viscosity(rates, strength[:, at])
            rows[8 * group : 8 * group + 8] = zeta[:8]
            rows[128 + 8 * group : 136 + 8 * group] = zeta[8:]
        top[6 + step] = zeta
        for at in range(8):
            zeta_out[step, HALO + at] = column_tile(lambda part: rows[part, :], at, 0)
            zeta_out[step, HALO + 8 + at] = column_tile(lambda part: rows[part, :], at, 1)

    @pl.loop(0, STEPS // 2)
    def _(turn):
        pltpu.make_async_copy(
            strains_hbm.at[pl.ds(2 * turn, 2)], strains.at[pl.ds(2 * turn, 2)], sems.at[5 + turn]
        ).wait()
        for part in range(2):
            cycle = 2 * turn + part
            cycle_zeta(cycle, STEPS - 1 - cycle, rows.at[part])

    lane = lax.broadcasted_iota(jnp.int32, (COLS, LANES), 1)
    row_at = lax.broadcasted_iota(jnp.int32, (COLS, LANES), 0)
    place = jnp.zeros((COLS, LANES), jnp.int32)
    for col in range(COLS):
        place = jnp.where(row_at == col, lax.rem(partner[col], COLS), place)
    strips = [jnp.where(lane == STRIP_PLACE, place.astype(jnp.float32), 0.0)] + [jnp.zeros((COLS, LANES), jnp.float32)] * (STRIP_PARTS - 1)
    for at in range(6 + STEPS):
        part, begin = (0, STRIP * at) if at < 6 else (1, STRIP * (at - 6))
        moved = pltpu.roll(top[at], (begin + STRIP) % LANES, 1)
        strips[part] = jnp.where((lane >= begin) & (lane < begin + STRIP), moved, strips[part])
    for k, at in enumerate((0, 1, 5)):
        moved = pltpu.roll(top[at], (STRIP_BEFORE + k + STRIP + 1) % LANES, 1)
        strips[0] = jnp.where(lane == STRIP_BEFORE + k, moved, strips[0])
    for part in range(STRIP_PARTS):
        own_out[0, part] = strips[part]
        strip_out[0, part] = strips[part].astype(bf16)


def join_kernel(count, *refs):
    out = refs[(len(refs) + count - 1) // 2]
    at = 0
    for part in refs[:count]:
        size = part.shape[0]
        out[at : at + size] = part[...]
        at += size


def fold_kernel(offsets, *refs):
    *parts, own, result, out, strips, turned, tiles, sems = refs
    copies = [
        pltpu.make_async_copy(result.at[:, pl.ds(at, 120), :], out.at[:, pl.ds(at, 120), :], sems.at[at // 128])
        for at in (0, 128)
    ]
    for copy in copies:
        copy.start()
    me = lax.axis_index("lon")
    blocks = strips.shape[0]
    total = blocks * COLS
    count = total // LANES
    order = iter(offsets)
    for part in parts:
        for k in range(part.shape[0]):
            strips[next(order)] = part[k].astype(jnp.float32)
    strips[0] = own[0]
    for part in range(STRIP_PARTS):
        for r in range(count):
            group = [strips[lax.bitwise_xor(me, 8 * r + k), part] for k in range(8)]
            turned[part, :, LANES * r : LANES * r + LANES] = jnp.concatenate(group, axis=0).T

    def field(at):
        part, begin = (0, STRIP * at) if at < 6 else (1, STRIP * (at - 6))
        return turned[part, begin : begin + STRIP, :]

    lane = lax.broadcasted_iota(jnp.int32, (8, LANES), 1)
    row = lax.broadcasted_iota(jnp.int32, (STRIP, total), 0)
    last = row == STRIP - 1
    far_row = lax.broadcasted_iota(jnp.int32, (8, total), 0) == 7
    places = [
        (7 - lane // COLS) * COLS
        + jnp.broadcast_to(
            turned[0, STRIP_PLACE : STRIP_PLACE + 1, LANES * r : LANES * r + LANES], (8, LANES)
        ).astype(jnp.int32)
        for r in range(count)
    ]

    west_places = [jnp.where(place == 0, LANES - 1, place - 1) for place in places]

    def gathered(value, r, place):
        part = value[STRIP - 8 :, LANES * (r % count) : LANES * (r % count) + LANES]
        return jnp.take_along_axis(part, place, axis=1, mode="promise_in_bounds")

    def by_partner(value):
        return jnp.concatenate([gathered(value, count - 1 - r, places[r]) for r in range(count)], axis=1)

    def by_partner_west(value):
        return jnp.concatenate(
            [
                jnp.where(
                    places[r] == 0,
                    gathered(value, count - 2 - r, west_places[r]),
                    gathered(value, count - 1 - r, west_places[r]),
                )
                for r in range(count)
            ],
            axis=1,
        )

    def at_fold(far):
        return jnp.concatenate([jnp.zeros((STRIP - 8, total), jnp.float32), jnp.where(far_row, far, 0.0)], axis=0)

    def next_col(value):
        return pltpu.roll(value, total - 1, 1)

    def prev_col(value):
        return pltpu.roll(value, 1, 1)

    def row_above(value):
        return jnp.where(last, 0.0, pltpu.roll(value, STRIP - 1, 0))

    def row_below(value):
        return pltpu.roll(value, 1, 0)

    vel_u, vel_v, one, two, shear, weight = (field(at) for at in range(6))
    before = turned[0, STRIP_BEFORE : STRIP_BEFORE + 8, :]
    wet = weight != 0.0
    next_weight = next_col(weight)
    far_weight = by_partner(weight)
    for step in range(STEPS):
        p = weight * vel_u
        q = weight * vel_v
        if step == 0:
            next_p, next_q, far_p, far_q = next_col(p), next_col(q), by_partner(p), by_partner(q)
        else:
            next_p = next_weight * (next_col(rest_u) + x)
            next_q = next_weight * (next_col(rest_v) + third)
            far_p = far_weight * (by_partner(rest_u) + by_partner_west(x))
            far_q = far_weight * (by_partner(rest_v) + by_partner_west(third))
        low_p = row_below(p)
        low_q = row_below(q)
        if step == 0:
            low_p = jnp.where(row == 0, before[2:3] * before[0:1], low_p)
            low_q = jnp.where(row == 0, before[2:3] * before[1:2], low_q)
        along = 0.5 * (p - next_p)
        across = 0.5 * (low_q - q + at_fold(far_q))
        one = one + (along + across)
        two = two + (along - across)
        shear = shear + (low_p - p - at_fold(far_p)) + (q - next_q)
        zeta = field(6 + step)
        first = zeta * one
        quarter = 0.25 * zeta
        second = quarter * two
        third = quarter * shear
        x = first + second
        y = first - second
        wet_u = jnp.where(wet, vel_u, 0.0)
        wet_v = jnp.where(wet, vel_v, 0.0)
        rest_u = (wet_u - 0.1 * wet_v) - x + (third - row_above(third))
        rest_v = (wet_v + 0.1 * wet_u) - third + (y - row_above(y))
        vel_u = rest_u + prev_col(x)
        vel_v = rest_v + prev_col(third)

    shift = lax.rem(total - COLS * me, total)
    rows = [pltpu.roll(value, shift, 1)[:, :LANES] for value in (vel_u, vel_v, one, two, shear)]
    rows.append(jnp.zeros((LANES - 80, LANES), jnp.float32))
    top = SHRINK * jnp.concatenate(rows, axis=0).T[:COLS]
    reached = lax.broadcasted_iota(jnp.int32, (COLS, LANES), 1) >= LANES - STEPS - 1
    for field in range(5):
        moved = pltpu.roll(top, LANES - 16 - 16 * field, 1)
        before = jnp.concatenate([result[field, 120:128, :], result[field, 248:256, :]], axis=0)
        tiles[field] = jnp.where(reached, moved, before)
    last_copies = [
        pltpu.make_async_copy(
            tiles.at[:, 8 * half : 8 * half + 8, :], out.at[:, pl.ds(128 * half + 120, 8), :], sems.at[2 + half]
        )
        for half in range(2)
    ]
    for copy in last_copies:
        copy.start()
    copies.extend(last_copies)
    for copy in copies:
        copy.wait()


def stepper(state, zeta, weight):
    vel_u, vel_v, one, two, shear = (state.at[field] for field in range(5))
    lane = lax.broadcasted_iota(jnp.int32, (8, LANES), 1)
    sub = lax.broadcasted_iota(jnp.int32, (8, LANES), 0)
    first_lane = lane == 0
    last_lane = lane == LANES - 1
    top = sub == 0
    bottom = sub == 7

    def row_above(value):
        turned = pltpu.roll(value, LANES - 1, 1)
        even, odd = turned[:8], turned[8:]
        carried = jnp.where(bottom, 0.0, pltpu.roll(even, 7, 0))
        return jnp.concatenate([jnp.where(last_lane, odd, even), jnp.where(last_lane, carried, odd)], 0)

    def row_below(value):
        turned = pltpu.roll(value, 1, 1)
        even, odd = turned[:8], turned[8:]
        carried = jnp.where(top, 0.0, pltpu.roll(odd, 1, 0))
        return jnp.concatenate([jnp.where(first_lane, carried, even), jnp.where(first_lane, even, odd)], 0)

    def forces(place, col):
        u, v, w = vel_u[place], vel_v[place], weight[col]
        wet = w != 0.0
        wet_u = jnp.where(wet, u, 0.0)
        wet_v = jnp.where(wet, v, 0.0)
        return w * u, w * v, wet_u - 0.1 * wet_v, wet_v + 0.1 * wet_u

    def strains_of(step, col, one_at, two_at, shear_at):
        z = zeta[step, col]
        first = z * one_at
        quarter = 0.25 * z
        second = quarter * two_at
        return first + second, quarter * shear_at, first - second

    def stored_strains(step, place, col):
        return strains_of(step, col, one[place], two[place], shear[place])

    def velocities(keep_u, keep_v, west_x, west_c, x, c, y):
        return keep_u + (west_x - x) + (c - row_above(c)), keep_v + (west_c - c) + (y - row_above(y))

    def advance(step, place, next_place, col, carry):
        p, q, keep_u, keep_v, west_x, west_c = carry
        next_p, next_q, next_u, next_v = forces(next_place, col + 1)
        along = 0.5 * (p - next_p)
        across = 0.5 * (row_below(q) - q)
        turn = row_below(p) - p
        new_one = one[place] + (along + across)
        new_two = two[place] + (along - across)
        new_shear = shear[place] + turn + (q - next_q)
        x, c, y = strains_of(step, col, new_one, new_two, new_shear)
        new_u, new_v = velocities(keep_u, keep_v, west_x, west_c, x, c, y)
        return (new_u, new_v, new_one, new_two, new_shear), (next_p, next_q, next_u, next_v, x, c)

    return forces, stored_strains, velocities, advance


def inner_steps(state, zeta, weight, steps):
    forces, _, _, advance = stepper(state, zeta, weight)
    blank = jnp.zeros((TILE, LANES), jnp.float32)
    for step in steps:
        begin = HALO + step
        carry = forces(begin, begin) + (blank, blank)
        for col in range(begin, HALO + COLS - 1 - step):
            new, carry = advance(step, col, col + 1, col, carry)
            for field in range(2 if col == begin else 0, 5):
                state[field, col] = new[field]


def first_inner_kernel(state_in, zeta, weight, state, west, east):
    inner_steps(state, zeta, weight, range(EDGE_SPLIT))
    for out, places, rests, shift in (
        (west, WEST_PLACES, WEST_RESTS, COLS),
        (east, EAST_PLACES, EAST_RESTS, -COLS),
    ):
        for entry, place in places.items():
            kind, which, col = entry
            source = {"state": state, "zeta": zeta}[kind].at[which] if kind != "mass" else weight
            tile = source[col + shift]
            sent = tile.astype(jnp.bfloat16)
            out[place] = sent
            if entry in rests:
                out[len(places) + rests.index(entry)] = (tile - sent.astype(jnp.float32)).astype(jnp.bfloat16)


def second_inner_kernel(state_in, zeta, weight, sides, state):
    inner_steps(state, zeta, weight, range(EDGE_SPLIT, STEPS))

    @pl.loop(0, 9)
    def _(at):
        for field in range(5):
            sides[field, HALO + at] = state[field, HALO + at]
            sides[field, EAST_END - HALO - 7 - at] = state[field, HALO + 7 + at]


def edge_kernel(west, east, state_in, zeta_in, mass_in, out, state, zeta, weight):
    for source, places, rests in ((west, WEST_PLACES, WEST_RESTS), (east, EAST_PLACES, EAST_RESTS)):
        for entry, place in places.items():
            kind, which, col = entry
            tile = source[place].astype(jnp.float32)
            if entry in rests:
                tile = tile + source[len(places) + rests.index(entry)].astype(jnp.float32)
            if kind == "state":
                state[which, EAST_END - col if col >= HALO + COLS else col] = tile
            elif kind == "mass":
                weight[col] = tile
            else:
                zeta[which, col] = tile

    forces, stored_strains, velocities, advance = stepper(state, zeta, weight)
    blank = jnp.zeros((TILE, LANES), jnp.float32)

    def grow(step):
        for middle in (HALO - 1, HALO + COLS - 1):
            cols = range(middle - step, middle + step + 1)
            at = [col if middle < HALO else EAST_END - col for col in (*cols, middle + step + 1)]
            behind = middle - step - 1
            x, c, _ = stored_strains(step, behind if middle < HALO else EAST_END - behind, behind)
            carry = forces(at[0], cols[0]) + (x, c)
            for part, col in enumerate(cols):
                new, carry = advance(step, at[part], at[part + 1], col, carry)
                for field in range(5):
                    state[field, at[part]] = new[field]
            ahead = middle + step + 1
            state[0, at[-1]], state[1, at[-1]] = velocities(*carry[2:], *stored_strains(step, at[-1], ahead))

    for step in range(EDGE_SPLIT):
        grow(step)

    start = EAST_END - (HALO + COLS - 1)

    @pl.loop(EDGE_SPLIT, STEPS)
    def _(step):
        begin = HALO + COLS - 1 - step
        x, c, _ = stored_strains(step, step + (start + 1), begin - 1)
        carry = forces(step + start, begin) + (x, c)
        west_carry = forces(step, step) + (blank, blank)
        for part in range(8):
            new, carry = advance(step, step + (start - part), step + (start - part - 1), begin + part, carry)
            west_new, west_carry = advance(step, step + part, step + part + 1, step + part, west_carry)
            for field in range(5):
                state[field, step + (start - part)] = new[field]
                state[field, step + part] = west_new[field]
        u, v = velocities(*west_carry[2:], *stored_strains(step, step + 8, step + 8))
        state[0, step + 8] = u
        state[1, step + 8] = v

    @pl.loop(0, 8)
    def _(at):
        for field in range(5):
            for half in range(2):
                tile = SHRINK * state[field, (HALO + at, EAST_END - HALO - 8 - at)[half]]
                even, odd = column_slices(at, half)
                out[field, even, :] = tile[:8]
                out[field, odd, :] = tile[8:]


def join(parts, passed):
    whole = pl.BlockSpec(memory_space=pltpu.VMEM)
    size = sum(part.shape[0] for part in parts)
    held, *passed = pl.pallas_call(
        functools.partial(join_kernel, len(parts)),
        out_shape=(
            jax.ShapeDtypeStruct((size, *parts[0].shape[1:]), parts[0].dtype),
            *(jax.ShapeDtypeStruct(x.shape, x.dtype) for x in passed),
        ),
        in_specs=[whole] * (len(parts) + len(passed)),
        out_specs=(whole,) * (1 + len(passed)),
        input_output_aliases={len(parts) + k: 1 + k for k in range(len(passed))},
        compiler_params=pltpu.CompilerParams(vmem_limit_bytes=16 * 1024 * 1024),
    )(*parts, *passed)
    return held, passed


def gather_stages(count):
    stages = [(1,)]
    bit = 4
    while bit < count:
        stages.append((2 * bit, 3 * bit, bit) if 2 * bit < count else (bit,))
        bit *= 4
    return stages + [(2,)]


def exchange(held, steps, count):
    return [held] + [lax.ppermute(held, "lon", [(i, i ^ step) for i in range(count)]) for step in steps]


def on_device(final_cot, strains, strength, mass, ice_mask, partner):
    count = lax.axis_size("lon")
    whole = pl.BlockSpec(memory_space=pltpu.VMEM)
    hbm = pl.BlockSpec(memory_space=pltpu.HBM)
    f32 = jnp.float32
    bf16 = jnp.bfloat16
    params = pltpu.CompilerParams(vmem_limit_bytes=16 * 1024 * 1024)
    cells = [
        pltpu.with_memory_space_constraint(x, pltpu.HBM)
        for x in (as_rows(final_cot), strains, strength, mass, ice_mask, partner)
    ]
    state_shape = cells[0].shape
    extended = (
        jax.ShapeDtypeStruct((5, EXT, TILE, LANES), f32),
        jax.ShapeDtypeStruct((STEPS, EXT, TILE, LANES), f32),
        jax.ShapeDtypeStruct((EXT, TILE, LANES), f32),
    )
    sends = (
        jax.ShapeDtypeStruct((WEST_SIZE, TILE, LANES), bf16),
        jax.ShapeDtypeStruct((EAST_SIZE, TILE, LANES), bf16),
    )
    strip, own_strip, state, zeta, weight = pl.pallas_call(
        pack_kernel,
        out_shape=(
            jax.ShapeDtypeStruct((1, STRIP_PARTS, COLS, LANES), bf16),
            jax.ShapeDtypeStruct((1, STRIP_PARTS, COLS, LANES), f32),
            *extended,
        ),
        in_specs=[hbm] * 6,
        out_specs=(whole,) * 5,
        scratch_shapes=[
            pltpu.VMEM(state_shape, f32),
            pltpu.VMEM(strains.shape, bf16),
            pltpu.VMEM(strength.shape, f32),
            pltpu.VMEM(mass.shape, f32),
            pltpu.VMEM(ice_mask.shape, jnp.int32),
            pltpu.SMEM(partner.shape, jnp.int32),
            pltpu.VMEM((2, 256, LANES), f32),
            pltpu.VMEM((6 + STEPS, COLS, LANES), f32),
            pltpu.SemaphoreType.DMA((5 + STEPS // 2,)),
        ],
        compiler_params=params,
    )(*cells)
    stages = gather_stages(count)
    offsets = [0]
    for steps in stages:
        offsets = [offset ^ step for step in (0, *steps) for offset in offsets]
    parts = exchange(strip, stages[0], count)
    state, west_send, east_send = pl.pallas_call(
        first_inner_kernel,
        out_shape=(extended[0], *sends),
        in_specs=[whole] * 3,
        out_specs=(whole,) * 3,
        input_output_aliases={0: 0},
        compiler_params=params,
    )(state, zeta, weight)
    held, (west_send, east_send) = join(parts, (west_send, east_send))
    west = lax.ppermute(west_send, "lon", [(i, (i + 1) % count) for i in range(count)])
    east = lax.ppermute(east_send, "lon", [(i, (i - 1) % count) for i in range(count)])
    state, _ = pl.pallas_call(
        second_inner_kernel,
        out_shape=(extended[0], extended[0]),
        in_specs=[whole] * 3,
        out_specs=(whole,) * 2,
        input_output_aliases={0: 1},
        compiler_params=params,
        cost_estimate=pl.CostEstimate(flops=1500000000, bytes_accessed=0, transcendentals=0),
    )(state, zeta, weight)
    for steps in stages[1:]:
        parts = exchange(held, steps, count)
        if steps != stages[-1]:
            held, (state,) = join(parts, (state,))
    out, *_ = pl.pallas_call(
        edge_kernel,
        out_shape=(jax.ShapeDtypeStruct(state_shape, f32), *extended),
        in_specs=[whole] * 5,
        out_specs=(whole,) * 4,
        input_output_aliases={2: 1, 3: 2, 4: 3},
        compiler_params=params,
    )(west, east, state, zeta, weight)
    out = pl.pallas_call(
        functools.partial(fold_kernel, offsets),
        out_shape=jax.ShapeDtypeStruct(state_shape, f32),
        in_specs=[whole] * (len(parts) + 2),
        out_specs=hbm,
        scratch_shapes=[
            pltpu.VMEM((count, STRIP_PARTS, COLS, LANES), f32),
            pltpu.VMEM((STRIP_PARTS, LANES, count * COLS), f32),
            pltpu.VMEM((5, COLS, LANES), f32),
            pltpu.SemaphoreType.DMA((4,)),
        ],
        compiler_params=params,
    )(*parts, own_strip, out)
    return from_rows(out)


def solution(mesh):
    return jax.shard_map(
        on_device,
        mesh=mesh,
        in_specs=(
            P("ens", "lon", None),
            P("ens", None, "lon", None),
            P("lon", None),
            P("lon", None),
            P("lon", None),
            P("lon"),
        ),
        out_specs=P("ens", "lon", None),
        check_vma=False,
    )
```

```python
import functools

import jax
import jax.numpy as jnp
from jax import lax
from jax.experimental import pallas as pl
from jax.experimental.pallas import tpu as pltpu
from jax.sharding import PartitionSpec as P

COLS = 16
STEPS = 8
HALO = 8
TILE = 16
LANES = 128
GROUPS = 16
EXT = 40
UNROLL = 8

WEST_COLS = [4, 5, 6, 7]
EAST_COLS = [24, 25, 26, 27]


def numbered(entries):
    return {entry: at for at, entry in enumerate(entries)}


WEST_PLACES = numbered(
    [("state", field, col) for field in range(5) for col in WEST_COLS]
    + [("state", field, 3) for field in range(2, 5)]
    + [("mass", 0, col) for col in WEST_COLS]
    + [
        ("zeta", step, col)
        for step in range(STEPS)
        for col in range(6 - step if step < 4 else step, 8)
    ]
)
EAST_PLACES = numbered(
    [("state", field, col) for field in range(5) for col in EAST_COLS]
    + [("mass", 0, col) for col in EAST_COLS]
    + [
        ("zeta", step, col)
        for step in range(STEPS)
        for col in range(24, 25 + step if step < 4 else 31 - step)
    ]
)
WEST_RESTS = [("state", field, 7) for field in range(2, 5)] + [("zeta", step, 7) for step in range(2)]
EAST_RESTS = [("state", 0, 24), ("state", 1, 24), ("mass", 0, 24)]
WEST_SIZE = len(WEST_PLACES) + len(WEST_RESTS)
EAST_SIZE = len(EAST_PLACES) + len(EAST_RESTS)
STRIP = 16
STRIP_PARTS = 2
STRIP_BEFORE = 6 * STRIP
STRIP_PLACE = STRIP_BEFORE + 8
EAST_END = EXT + 7
EDGE_SPLIT = 4
SHRINK = (5.0 / 6.0) ** STEPS


def as_rows(field):
    lead = field.shape[:-2]
    tiled = field.reshape(lead + (2, 8, GROUPS, LANES)).swapaxes(-3, -2)
    return tiled.reshape(lead + (2 * GROUPS * 8, LANES))


def from_rows(field):
    lead = field.shape[:-2]
    tiled = field.reshape(lead + (2, GROUPS, 8, LANES)).swapaxes(-3, -2)
    return tiled.reshape(lead + (COLS, GROUPS * LANES))


def column_slices(col, half):
    start = half * 128 + col
    return pl.ds(start, 8, 16), pl.ds(start + 8, 8, 16)


def column_tile(load, col, half):
    even, odd = column_slices(col, half)
    return jnp.concatenate([load(even), load(odd)], axis=0)


def viscosity(rates, strength):
    square = rates[0] * rates[0] + 0.25 * (rates[1] * rates[1] + rates[2] * rates[2])
    return (0.1 * strength) * lax.rsqrt(jnp.maximum(square, 0.25))


def pack_kernel(
    state_hbm, strains_hbm, strength_hbm, mass_hbm, mask_hbm, partner_hbm,
    strip_out, own_out, state_out, zeta_out, mass_out,
    state, strains, strength, mass, mask, partner, rows, top, sems,
):
    bf16 = jnp.bfloat16
    cell_copies = [
        pltpu.make_async_copy(mass_hbm, mass, sems.at[0]),
        pltpu.make_async_copy(mask_hbm, mask, sems.at[1]),
    ]
    state_copy = pltpu.make_async_copy(state_hbm, state, sems.at[2])
    first_copies = [
        pltpu.make_async_copy(strength_hbm, strength, sems.at[3]),
        pltpu.make_async_copy(partner_hbm, partner, sems.at[4]),
    ]
    strain_copies = [
        pltpu.make_async_copy(strains_hbm.at[2 * k : 2 * k + 2], strains.at[2 * k : 2 * k + 2], sems.at[5 + k])
        for k in range(STEPS // 2)
    ]
    for copy in [*first_copies, *strain_copies, *cell_copies, state_copy]:
        copy.start()

    for copy in first_copies:
        copy.wait()

    def cycle_zeta(cycle, step, rows):
        for group in range(GROUPS):
            at = slice(LANES * group, LANES * group + LANES)
            rates = [strains[cycle, k, :, at].astype(jnp.float32) for k in range(3)]
            zeta = viscosity(rates, strength[:, at])
            rows[8 * group : 8 * group + 8] = zeta[:8]
            rows[128 + 8 * group : 136 + 8 * group] = zeta[8:]
        top[6 + step] = zeta
        for at in range(8):
            zeta_out[step, HALO + at] = column_tile(lambda part: rows[part, :], at, 0)
            zeta_out[step, HALO + 8 + at] = column_tile(lambda part: rows[part, :], at, 1)

    @pl.loop(0, STEPS // 2)
    def _(turn):
        pltpu.make_async_copy(
            strains_hbm.at[pl.ds(2 * turn, 2)], strains.at[pl.ds(2 * turn, 2)], sems.at[5 + turn]
        ).wait()
        for part in range(2):
            cycle = 2 * turn + part
            cycle_zeta(cycle, STEPS - 1 - cycle, rows.at[part])

    for copy in cell_copies:
        copy.wait()
    for group in range(GROUPS):
        at = slice(LANES * group, LANES * group + LANES)
        weight = mask[:, at].astype(jnp.float32) / (6.0 * mass[:, at])
        rows[0, 8 * group : 8 * group + 8] = weight[:8]
        rows[0, 128 + 8 * group : 136 + 8 * group] = weight[8:]
    top[5] = weight
    for at in range(8):
        tile = column_tile(lambda part: rows[0, part, :], at, 0)
        mass_out[HALO + at] = tile
        tile = column_tile(lambda part: rows[0, part, :], at, 1)
        mass_out[HALO + 8 + at] = tile
    state_copy.wait()

    @pl.loop(0, 8)
    def _(at):
        for field in range(5):
            state_out[field, HALO + at] = column_tile(lambda part: state[field, part, :], at, 0)
            state_out[field, HALO + 8 + at] = column_tile(lambda part: state[field, part, :], at, 1)

    for field in range(5):
        top[field, :8] = state[field, 120:128, :]
        top[field, 8:] = state[field, 248:256, :]
    lane = lax.broadcasted_iota(jnp.int32, (COLS, LANES), 1)
    row_at = lax.broadcasted_iota(jnp.int32, (COLS, LANES), 0)
    place = jnp.zeros((COLS, LANES), jnp.int32)
    for col in range(COLS):
        place = jnp.where(row_at == col, lax.rem(partner[col], COLS), place)
    strips = [jnp.where(lane == STRIP_PLACE, place.astype(jnp.float32), 0.0)] + [jnp.zeros((COLS, LANES), jnp.float32)] * (STRIP_PARTS - 1)
    for at in range(6 + STEPS):
        part, begin = (0, STRIP * at) if at < 6 else (1, STRIP * (at - 6))
        moved = pltpu.roll(top[at], (begin + STRIP) % LANES, 1)
        strips[part] = jnp.where((lane >= begin) & (lane < begin + STRIP), moved, strips[part])
    for k, at in enumerate((0, 1, 5)):
        moved = pltpu.roll(top[at], (STRIP_BEFORE + k + STRIP + 1) % LANES, 1)
        strips[0] = jnp.where(lane == STRIP_BEFORE + k, moved, strips[0])
    for part in range(STRIP_PARTS):
        own_out[0, part] = strips[part]
        strip_out[0, part] = strips[part].astype(bf16)


def join_kernel(count, *refs):
    out = refs[(len(refs) + count - 1) // 2]
    at = 0
    for part in refs[:count]:
        size = part.shape[0]
        out[at : at + size] = part[...]
        at += size


def fold_kernel(offsets, *refs):
    *parts, own, result, out, strips, turned, tiles, sems = refs
    copies = [
        pltpu.make_async_copy(result.at[:, pl.ds(at, 120), :], out.at[:, pl.ds(at, 120), :], sems.at[at // 128])
        for at in (0, 128)
    ]
    for copy in copies:
        copy.start()
    me = lax.axis_index("lon")
    blocks = strips.shape[0]
    total = blocks * COLS
    count = total // LANES
    order = iter(offsets)
    for part in parts:
        for k in range(part.shape[0]):
            strips[next(order)] = part[k].astype(jnp.float32)
    strips[0] = own[0]
    for part in range(STRIP_PARTS):
        for r in range(count):
            group = [strips[lax.bitwise_xor(me, 8 * r + k), part] for k in range(8)]
            turned[part, :, LANES * r : LANES * r + LANES] = jnp.concatenate(group, axis=0).T

    def field(at):
        part, begin = (0, STRIP * at) if at < 6 else (1, STRIP * (at - 6))
        return turned[part, begin : begin + STRIP, :]

    lane = lax.broadcasted_iota(jnp.int32, (8, LANES), 1)
    row = lax.broadcasted_iota(jnp.int32, (STRIP, total), 0)
    last = row == STRIP - 1
    far_row = lax.broadcasted_iota(jnp.int32, (8, total), 0) == 7
    places = [
        (7 - lane // COLS) * COLS
        + jnp.broadcast_to(
            turned[0, STRIP_PLACE : STRIP_PLACE + 1, LANES * r : LANES * r + LANES], (8, LANES)
        ).astype(jnp.int32)
        for r in range(count)
    ]

    west_places = [jnp.where(place == 0, LANES - 1, place - 1) for place in places]

    def gathered(value, r, place):
        part = value[STRIP - 8 :, LANES * (r % count) : LANES * (r % count) + LANES]
        return jnp.take_along_axis(part, place, axis=1, mode="promise_in_bounds")

    def by_partner(value):
        return jnp.concatenate([gathered(value, count - 1 - r, places[r]) for r in range(count)], axis=1)

    def by_partner_west(value):
        return jnp.concatenate(
            [
                jnp.where(
                    places[r] == 0,
                    gathered(value, count - 2 - r, west_places[r]),
                    gathered(value, count - 1 - r, west_places[r]),
                )
                for r in range(count)
            ],
            axis=1,
        )

    def at_fold(far):
        return jnp.concatenate([jnp.zeros((STRIP - 8, total), jnp.float32), jnp.where(far_row, far, 0.0)], axis=0)

    def next_col(value):
        return pltpu.roll(value, total - 1, 1)

    def prev_col(value):
        return pltpu.roll(value, 1, 1)

    def row_above(value):
        return jnp.where(last, 0.0, pltpu.roll(value, STRIP - 1, 0))

    def row_below(value):
        return pltpu.roll(value, 1, 0)

    vel_u, vel_v, one, two, shear, weight = (field(at) for at in range(6))
    before = turned[0, STRIP_BEFORE : STRIP_BEFORE + 8, :]
    wet = weight != 0.0
    next_weight = next_col(weight)
    far_weight = by_partner(weight)
    for step in range(STEPS):
        p = weight * vel_u
        q = weight * vel_v
        if step == 0:
            next_p, next_q, far_p, far_q = next_col(p), next_col(q), by_partner(p), by_partner(q)
        else:
            next_p = next_weight * (next_col(rest_u) + x)
            next_q = next_weight * (next_col(rest_v) + third)
            far_p = far_weight * (by_partner(rest_u) + by_partner_west(x))
            far_q = far_weight * (by_partner(rest_v) + by_partner_west(third))
        low_p = row_below(p)
        low_q = row_below(q)
        if step == 0:
            low_p = jnp.where(row == 0, before[2:3] * before[0:1], low_p)
            low_q = jnp.where(row == 0, before[2:3] * before[1:2], low_q)
        along = 0.5 * (p - next_p)
        across = 0.5 * (low_q - q + at_fold(far_q))
        one = one + (along + across)
        two = two + (along - across)
        shear = shear + (low_p - p - at_fold(far_p)) + (q - next_q)
        zeta = field(6 + step)
        first = zeta * one
        quarter = 0.25 * zeta
        second = quarter * two
        third = quarter * shear
        x = first + second
        y = first - second
        wet_u = jnp.where(wet, vel_u, 0.0)
        wet_v = jnp.where(wet, vel_v, 0.0)
        rest_u = (wet_u - 0.1 * wet_v) - x + (third - row_above(third))
        rest_v = (wet_v + 0.1 * wet_u) - third + (y - row_above(y))
        vel_u = rest_u + prev_col(x)
        vel_v = rest_v + prev_col(third)

    shift = lax.rem(total - COLS * me, total)
    rows = [pltpu.roll(value, shift, 1)[:, :LANES] for value in (vel_u, vel_v, one, two, shear)]
    rows.append(jnp.zeros((LANES - 80, LANES), jnp.float32))
    top = SHRINK * jnp.concatenate(rows, axis=0).T[:COLS]
    reached = lax.broadcasted_iota(jnp.int32, (COLS, LANES), 1) >= LANES - STEPS - 1
    for field in range(5):
        moved = pltpu.roll(top, LANES - 16 - 16 * field, 1)
        before = jnp.concatenate([result[field, 120:128, :], result[field, 248:256, :]], axis=0)
        tiles[field] = jnp.where(reached, moved, before)
    last_copies = [
        pltpu.make_async_copy(
            tiles.at[:, 8 * half : 8 * half + 8, :], out.at[:, pl.ds(128 * half + 120, 8), :], sems.at[2 + half]
        )
        for half in range(2)
    ]
    for copy in last_copies:
        copy.start()
    copies.extend(last_copies)
    for copy in copies:
        copy.wait()


def stepper(state, zeta, weight):
    vel_u, vel_v, one, two, shear = (state.at[field] for field in range(5))
    lane = lax.broadcasted_iota(jnp.int32, (8, LANES), 1)
    sub = lax.broadcasted_iota(jnp.int32, (8, LANES), 0)
    first_lane = lane == 0
    last_lane = lane == LANES - 1
    top = sub == 0
    bottom = sub == 7

    def row_above(value):
        turned = pltpu.roll(value, LANES - 1, 1)
        even, odd = turned[:8], turned[8:]
        carried = jnp.where(bottom, 0.0, pltpu.roll(even, 7, 0))
        return jnp.concatenate([jnp.where(last_lane, odd, even), jnp.where(last_lane, carried, odd)], 0)

    def row_below(value):
        turned = pltpu.roll(value, 1, 1)
        even, odd = turned[:8], turned[8:]
        carried = jnp.where(top, 0.0, pltpu.roll(odd, 1, 0))
        return jnp.concatenate([jnp.where(first_lane, carried, even), jnp.where(first_lane, even, odd)], 0)

    def forces(place, col):
        u, v, w = vel_u[place], vel_v[place], weight[col]
        wet = w != 0.0
        wet_u = jnp.where(wet, u, 0.0)
        wet_v = jnp.where(wet, v, 0.0)
        return w * u, w * v, wet_u - 0.1 * wet_v, wet_v + 0.1 * wet_u

    def strains_of(step, col, one_at, two_at, shear_at):
        z = zeta[step, col]
        first = z * one_at
        quarter = 0.25 * z
        second = quarter * two_at
        return first + second, quarter * shear_at, first - second

    def stored_strains(step, place, col):
        return strains_of(step, col, one[place], two[place], shear[place])

    def velocities(keep_u, keep_v, west_x, west_c, x, c, y):
        return keep_u + (west_x - x) + (c - row_above(c)), keep_v + (west_c - c) + (y - row_above(y))

    def advance(step, place, next_place, col, carry):
        p, q, keep_u, keep_v, west_x, west_c = carry
        next_p, next_q, next_u, next_v = forces(next_place, col + 1)
        along = 0.5 * (p - next_p)
        across = 0.5 * (row_below(q) - q)
        turn = row_below(p) - p
        new_one = one[place] + (along + across)
        new_two = two[place] + (along - across)
        new_shear = shear[place] + turn + (q - next_q)
        x, c, y = strains_of(step, col, new_one, new_two, new_shear)
        new_u, new_v = velocities(keep_u, keep_v, west_x, west_c, x, c, y)
        return (new_u, new_v, new_one, new_two, new_shear), (next_p, next_q, next_u, next_v, x, c)

    return forces, stored_strains, velocities, advance


def inner_steps(state, zeta, weight, steps):
    forces, _, _, advance = stepper(state, zeta, weight)
    blank = jnp.zeros((TILE, LANES), jnp.float32)
    for step in steps:
        begin = HALO + step
        carry = forces(begin, begin) + (blank, blank)
        for col in range(begin, HALO + COLS - 1 - step):
            new, carry = advance(step, col, col + 1, col, carry)
            for field in range(2 if col == begin else 0, 5):
                state[field, col] = new[field]


def first_inner_kernel(state_in, zeta, weight, state, west, east):
    inner_steps(state, zeta, weight, range(EDGE_SPLIT))
    for out, places, rests, shift in (
        (west, WEST_PLACES, WEST_RESTS, COLS),
        (east, EAST_PLACES, EAST_RESTS, -COLS),
    ):
        for entry, place in places.items():
            kind, which, col = entry
            source = {"state": state, "zeta": zeta}[kind].at[which] if kind != "mass" else weight
            tile = source[col + shift]
            sent = tile.astype(jnp.bfloat16)
            out[place] = sent
            if entry in rests:
                out[len(places) + rests.index(entry)] = (tile - sent.astype(jnp.float32)).astype(jnp.bfloat16)


def second_inner_kernel(state_in, zeta, weight, sides, state):
    inner_steps(state, zeta, weight, range(EDGE_SPLIT, STEPS))

    @pl.loop(0, 9)
    def _(at):
        for field in range(5):
            sides[field, HALO + at] = state[field, HALO + at]
            sides[field, EAST_END - HALO - 7 - at] = state[field, HALO + 7 + at]


def edge_kernel(west, east, state_in, zeta_in, mass_in, out, state, zeta, weight):
    for source, places, rests in ((west, WEST_PLACES, WEST_RESTS), (east, EAST_PLACES, EAST_RESTS)):
        for entry, place in places.items():
            kind, which, col = entry
            tile = source[place].astype(jnp.float32)
            if entry in rests:
                tile = tile + source[len(places) + rests.index(entry)].astype(jnp.float32)
            if kind == "state":
                state[which, EAST_END - col if col >= HALO + COLS else col] = tile
            elif kind == "mass":
                weight[col] = tile
            else:
                zeta[which, col] = tile

    forces, stored_strains, velocities, advance = stepper(state, zeta, weight)
    blank = jnp.zeros((TILE, LANES), jnp.float32)

    def grow(step):
        for middle in (HALO - 1, HALO + COLS - 1):
            cols = range(middle - step, middle + step + 1)
            at = [col if middle < HALO else EAST_END - col for col in (*cols, middle + step + 1)]
            behind = middle - step - 1
            x, c, _ = stored_strains(step, behind if middle < HALO else EAST_END - behind, behind)
            carry = forces(at[0], cols[0]) + (x, c)
            for part, col in enumerate(cols):
                new, carry = advance(step, at[part], at[part + 1], col, carry)
                for field in range(5):
                    state[field, at[part]] = new[field]
            ahead = middle + step + 1
            state[0, at[-1]], state[1, at[-1]] = velocities(*carry[2:], *stored_strains(step, at[-1], ahead))

    for step in range(EDGE_SPLIT):
        grow(step)

    start = EAST_END - (HALO + COLS - 1)

    @pl.loop(EDGE_SPLIT, STEPS)
    def _(step):
        begin = HALO + COLS - 1 - step
        x, c, _ = stored_strains(step, step + (start + 1), begin - 1)
        carry = forces(step + start, begin) + (x, c)
        west_carry = forces(step, step) + (blank, blank)
        for part in range(8):
            new, carry = advance(step, step + (start - part), step + (start - part - 1), begin + part, carry)
            west_new, west_carry = advance(step, step + part, step + part + 1, step + part, west_carry)
            for field in range(5):
                state[field, step + (start - part)] = new[field]
                state[field, step + part] = west_new[field]
        u, v = velocities(*west_carry[2:], *stored_strains(step, step + 8, step + 8))
        state[0, step + 8] = u
        state[1, step + 8] = v

    @pl.loop(0, 8)
    def _(at):
        for field in range(5):
            for half in range(2):
                tile = SHRINK * state[field, (HALO + at, EAST_END - HALO - 8 - at)[half]]
                even, odd = column_slices(at, half)
                out[field, even, :] = tile[:8]
                out[field, odd, :] = tile[8:]


def join(parts, passed):
    whole = pl.BlockSpec(memory_space=pltpu.VMEM)
    size = sum(part.shape[0] for part in parts)
    held, *passed = pl.pallas_call(
        functools.partial(join_kernel, len(parts)),
        out_shape=(
            jax.ShapeDtypeStruct((size, *parts[0].shape[1:]), parts[0].dtype),
            *(jax.ShapeDtypeStruct(x.shape, x.dtype) for x in passed),
        ),
        in_specs=[whole] * (len(parts) + len(passed)),
        out_specs=(whole,) * (1 + len(passed)),
        input_output_aliases={len(parts) + k: 1 + k for k in range(len(passed))},
        compiler_params=pltpu.CompilerParams(vmem_limit_bytes=16 * 1024 * 1024),
    )(*parts, *passed)
    return held, passed


def gather_stages(count):
    stages = [(1,)]
    bit = 4
    while bit < count:
        stages.append((2 * bit, 3 * bit, bit) if 2 * bit < count else (bit,))
        bit *= 4
    return stages + [(2,)]


def exchange(held, steps, count):
    return [held] + [lax.ppermute(held, "lon", [(i, i ^ step) for i in range(count)]) for step in steps]


def on_device(final_cot, strains, strength, mass, ice_mask, partner):
    count = lax.axis_size("lon")
    whole = pl.BlockSpec(memory_space=pltpu.VMEM)
    hbm = pl.BlockSpec(memory_space=pltpu.HBM)
    f32 = jnp.float32
    bf16 = jnp.bfloat16
    params = pltpu.CompilerParams(vmem_limit_bytes=16 * 1024 * 1024)
    cells = [
        pltpu.with_memory_space_constraint(x, pltpu.HBM)
        for x in (as_rows(final_cot), strains, strength, mass, ice_mask, partner)
    ]
    state_shape = cells[0].shape
    extended = (
        jax.ShapeDtypeStruct((5, EXT, TILE, LANES), f32),
        jax.ShapeDtypeStruct((STEPS, EXT, TILE, LANES), f32),
        jax.ShapeDtypeStruct((EXT, TILE, LANES), f32),
    )
    sends = (
        jax.ShapeDtypeStruct((WEST_SIZE, TILE, LANES), bf16),
        jax.ShapeDtypeStruct((EAST_SIZE, TILE, LANES), bf16),
    )
    strip, own_strip, state, zeta, weight = pl.pallas_call(
        pack_kernel,
        out_shape=(
            jax.ShapeDtypeStruct((1, STRIP_PARTS, COLS, LANES), bf16),
            jax.ShapeDtypeStruct((1, STRIP_PARTS, COLS, LANES), f32),
            *extended,
        ),
        in_specs=[hbm] * 6,
        out_specs=(whole,) * 5,
        scratch_shapes=[
            pltpu.VMEM(state_shape, f32),
            pltpu.VMEM(strains.shape, bf16),
            pltpu.VMEM(strength.shape, f32),
            pltpu.VMEM(mass.shape, f32),
            pltpu.VMEM(ice_mask.shape, jnp.int32),
            pltpu.SMEM(partner.shape, jnp.int32),
            pltpu.VMEM((2, 256, LANES), f32),
            pltpu.VMEM((6 + STEPS, COLS, LANES), f32),
            pltpu.SemaphoreType.DMA((5 + STEPS // 2,)),
        ],
        compiler_params=params,
    )(*cells)
    stages = gather_stages(count)
    offsets = [0]
    for steps in stages:
        offsets = [offset ^ step for step in (0, *steps) for offset in offsets]
    parts = exchange(strip, stages[0], count)
    state, west_send, east_send = pl.pallas_call(
        first_inner_kernel,
        out_shape=(extended[0], *sends),
        in_specs=[whole] * 3,
        out_specs=(whole,) * 3,
        input_output_aliases={0: 0},
        compiler_params=params,
    )(state, zeta, weight)
    held, (west_send, east_send) = join(parts, (west_send, east_send))
    west = lax.ppermute(west_send, "lon", [(i, (i + 1) % count) for i in range(count)])
    east = lax.ppermute(east_send, "lon", [(i, (i - 1) % count) for i in range(count)])
    state, _ = pl.pallas_call(
        second_inner_kernel,
        out_shape=(extended[0], extended[0]),
        in_specs=[whole] * 3,
        out_specs=(whole,) * 2,
        input_output_aliases={0: 1},
        compiler_params=params,
        cost_estimate=pl.CostEstimate(flops=1500000000, bytes_accessed=0, transcendentals=0),
    )(state, zeta, weight)
    for steps in stages[1:]:
        parts = exchange(held, steps, count)
        if steps != stages[-1]:
            held, (state,) = join(parts, (state,))
    out, *_ = pl.pallas_call(
        edge_kernel,
        out_shape=(jax.ShapeDtypeStruct(state_shape, f32), *extended),
        in_specs=[whole] * 5,
        out_specs=(whole,) * 4,
        input_output_aliases={2: 1, 3: 2, 4: 3},
        compiler_params=params,
    )(west, east, state, zeta, weight)
    out = pl.pallas_call(
        functools.partial(fold_kernel, offsets),
        out_shape=jax.ShapeDtypeStruct(state_shape, f32),
        in_specs=[whole] * (len(parts) + 2),
        out_specs=hbm,
        scratch_shapes=[
            pltpu.VMEM((count, STRIP_PARTS, COLS, LANES), f32),
            pltpu.VMEM((STRIP_PARTS, LANES, count * COLS), f32),
            pltpu.VMEM((5, COLS, LANES), f32),
            pltpu.SemaphoreType.DMA((4,)),
        ],
        compiler_params=params,
    )(*parts, own_strip, out)
    return from_rows(out)


def solution(mesh):
    return jax.shard_map(
        on_device,
        mesh=mesh,
        in_specs=(
            P("ens", "lon", None),
            P("ens", None, "lon", None),
            P("lon", None),
            P("lon", None),
            P("lon", None),
            P("lon"),
        ),
        out_specs=P("ens", "lon", None),
        check_vma=False,
    )
```
